1024 devices in a mesh: dp: 16 (over x, y), opt: 64 (over z, core).
Axes of the slice: x: 4, y: 4, z: 32, core: 2. Of those that a mesh axis runs over, the one named last changes fastest.
Arguments:
- gradients: bfloat16 [16, 128, 512, 512], P('dp', 'opt'), may hold values from -0.59765625 to 0.59765625
- owner_map: int32 [128], replicated, may hold values from 0 to 63, as said below
- left_root: bfloat16 [320, 512, 512], P('opt', 'dp'), may hold values from -0.25 to 0.25
- right_basis: bfloat16 [320, 512, 512], P('opt'), may hold values from -0.25 to 0.25
- right_eigen: float32 [320, 512], P('opt'), may hold values from 0.01 to 100
- left_stat: float32 [320, 512, 512], P('opt', 'dp'), may hold values from -6 to 6
- right_stat: float32 [320, 512, 512], P('opt', 'dp'), may hold values from -6 to 6
Outputs:
- update: bfloat16 [320, 512, 512], P('opt')
- left_new: float32 [320, 512, 512], P('opt', 'dp')
- right_new: float32 [320, 512, 512], P('opt', 'dp')
The draws below stay inside these ranges and needn't reach their ends.
Inputs may be any that keep to these rules, and one draw needn't show every extreme that they name: `owner_map`: blocks 2 * i to 2 * i + 1 go to different owners; no owner holds more than 5 blocks, and some owner holds exactly 5.
All inputs are finite; a program needn't handle non-finite values.
Results may differ from the reference program's by a relative error of at most 0.023.
Values may be sent and summed in bfloat16 or wider, within the bound.
No kernel may reach another device: no remote copies, remote signals or barrier semaphores. Data moves between devices by JAX's collectives and lax.ppermute only.
A program may use at most 32 MiB of HBM per device.

```python
import math
import jax
import jax.numpy as jnp
from jax import lax

B = 512
BLK = 2
CAP = 5
NBLK = 128
SLOTS = 320
N_DP = 16
N_OPT = 64


def draw_owner_map(key, part):
    key = jax.random.fold_in(key, 11)
    first_key, second_key = jax.random.split(key)
    senders = jax.random.permutation(first_key, N_OPT).astype(jnp.int32)
    owners = jax.random.permutation(second_key, N_OPT).astype(jnp.int32)
    heavy = max(1, N_OPT // 16)
    sources = heavy * (CAP - 1)
    ranks = jnp.arange(N_OPT, dtype=jnp.int32)
    second = jnp.where(ranks < sources, N_OPT - 1 - ranks // (CAP - 1), ranks - sources).astype(jnp.int32)
    pairs = jnp.stack([owners[ranks], owners[second]], axis=1)
    table = jnp.zeros((N_OPT, BLK), jnp.int32).at[senders].set(pairs)
    return table.reshape(N_OPT * BLK).astype(jnp.int32)


def spiked(values, own_key, source, target, blocks, factor):
    def block_of(axis_at):
        return (jnp.arange(values.shape[axis_at]) // (values.shape[axis_at] // blocks)).reshape((-1,) + (1,) * (values.ndim - 1 - axis_at))

    one_side = jax.random.permutation(own_key, blocks)[block_of(target)]
    other_side = (block_of(target) + blocks // 2) % blocks
    return jnp.where((block_of(source) == one_side) | (block_of(source) == other_side), factor * values, values)


def levels(rng, extent, shards, low, largest):
    level, own = 1.0, jax.random.fold_in(rng, 6)
    for axis_at, parts in shards:
        draws = jnp.exp(jax.random.uniform(jax.random.fold_in(own, axis_at), (parts,), jnp.float32, low / len(shards), largest / len(shards)))
        level = level * jnp.repeat(draws, extent[axis_at] // parts).reshape([-1 if axis == axis_at else 1 for axis in range(len(extent))])
    return level


def centred(stream_key, dims, width, limit, cuts=(), kind=jnp.bfloat16):
    loudness = levels(stream_key, dims, cuts, -0.22, 0.18) if cuts else 1.0
    entries = jax.random.normal(stream_key, dims, jnp.float32) * width * loudness
    return jnp.minimum(jnp.maximum(entries, -limit), limit).astype(kind)


def bell_draw_with(key, dims, scale, most, pieces, heavy, kind=jnp.bfloat16):
    entries = scale * jax.random.normal(key, dims, jnp.float32)
    if pieces:
        entries = entries * levels(key, dims, pieces, -0.22, 0.18)
    return jnp.clip(spiked(entries, jax.random.fold_in(key, 3), *heavy), -most, most).astype(kind)


def setup_inputs(seed: int = 0) -> dict:
    arg_keys = jax.random.split(jax.random.key(seed), 8)
    gradients = bell_draw_with(arg_keys[0], (N_DP, NBLK, B, B), 0.1, 0.59765625, ((0, 16), (1, 64)), (0, 2, 16, 2.0))
    owner_map = draw_owner_map(jax.random.fold_in(arg_keys[7], 71), 0)
    left_root = centred(arg_keys[2], (SLOTS, B, B), B ** -0.5, 0.25, ((0, 64), (1, 16)))
    right_basis = centred(arg_keys[3], (SLOTS, B, B), B ** -0.5, 0.25, ((0, 64),))
    right_eigen = jnp.clip(jnp.exp(math.log(100.0) - 9.2103404 * jax.random.uniform(arg_keys[4], (SLOTS, B), jnp.float32) ** levels(arg_keys[4], (SLOTS, B), ((0, 64),), -0.2, 0.2)), 0.01, 100.0)
    left_stat = centred(arg_keys[5], (SLOTS, B, B), 1.0, 6.0, ((0, 64), (1, 16)), jnp.float32)
    right_stat = centred(arg_keys[6], (SLOTS, B, B), 1.0, 6.0, ((0, 64), (1, 16)), jnp.float32)
    return {"gradients": gradients, "owner_map": owner_map, "left_root": left_root, "right_basis": right_basis, "right_eigen": right_eigen, "left_stat": left_stat, "right_stat": right_stat}


decay_rate = 0.9
epsilon = 1e-6


def reference(gradients, owner_map, left_root, right_basis, right_eigen, left_stat, right_stat):
    summed = jnp.sum(gradients.astype(jnp.float32), axis=0).astype(jnp.bfloat16)
    onehot = (owner_map[:, None] == jnp.arange(N_OPT, dtype=jnp.int32)[None, :]).astype(jnp.int32)
    earlier = jnp.cumsum(onehot, axis=0) - onehot
    slot_index = jnp.sum(earlier * onehot, axis=1).astype(jnp.int32)
    destination = (owner_map * CAP + slot_index).astype(jnp.int32)
    slotted = jnp.zeros((N_OPT * CAP, B, B), jnp.bfloat16).at[destination].set(summed)

    def precondition(items):
        block, root, basis, eigen, lstat, rstat = items
        left_gram = jnp.dot(block, block.T, preferred_element_type=jnp.float32)
        right_gram = jnp.dot(block.T, block, preferred_element_type=jnp.float32)
        left_applied = jnp.dot(root, block, preferred_element_type=jnp.float32).astype(jnp.bfloat16)
        factor = (eigen + epsilon) ** -0.25
        scaled = (jnp.dot(left_applied, basis, preferred_element_type=jnp.float32) * factor[None, :]).astype(jnp.bfloat16)
        update = jnp.dot(scaled, basis.T, preferred_element_type=jnp.float32).astype(jnp.bfloat16)
        left_new = decay_rate * lstat + (1.0 - decay_rate) * left_gram
        right_new = decay_rate * rstat + (1.0 - decay_rate) * right_gram
        return update, left_new, right_new

    update, left_new, right_new = lax.map(precondition, (slotted, left_root, right_basis, right_eigen, left_stat, right_stat))
    return update, left_new, right_new
```

```python
import jax
import jax.numpy as jnp
from jax import lax
from jax.sharding import Mesh, PartitionSpec as P

decay_rate = 0.9
epsilon = 1e-06
NEAR = 4


def broadcast_gather(x, axis):
    n = lax.axis_size(axis)
    copies = jnp.broadcast_to(x[None], (n,) + x.shape)
    return lax.all_to_all(copies, axis, split_axis=0, concat_axis=0, tiled=True)


def body(gradients, owner_map, left_root, right_basis, right_eigen, left_stat, right_stat):
    n_dp, n_far, n_near = lax.axis_size("dp"), lax.axis_size("far"), lax.axis_size("near")
    _, blocks, width, _ = gradients.shape
    cap, rows, _ = left_stat.shape
    my_dp, my_near = lax.axis_index("dp"), lax.axis_index("near")
    row_tiles, col_tiles = rows // 8, width // 128

    root = lax.all_gather(left_root, "dp", axis=1, tiled=True)

    sent = gradients.reshape(blocks, n_dp, row_tiles, 8, col_tiles, 128)
    sent = sent.transpose(1, 2, 4, 0, 3, 5).reshape(n_dp, n_far, blocks * 8, 128)
    parts = lax.all_to_all(sent, "dp", split_axis=0, concat_axis=0, tiled=True)
    summed = jnp.sum(parts.astype(jnp.float32), axis=0).astype(jnp.bfloat16)

    spread = lax.all_to_all(summed, "far", split_axis=0, concat_axis=0, tiled=True)
    tiles = broadcast_gather(spread, "near")
    tiles = tiles.reshape(n_near, n_far, blocks, 8, 128)

    owners = owner_map
    same = owners[:, None] == owners[None, :]
    order = jnp.arange(owners.shape[0], dtype=jnp.int32)
    slot = jnp.sum((same & (order[None, :] < order[:, None])).astype(jnp.int32), axis=1)
    place = jnp.where(owners % n_near == my_near, owners // n_near * cap + slot, -1)
    place = place.reshape(n_far, n_near, blocks).transpose(1, 0, 2).reshape(-1)
    pick = (jnp.arange(n_far * cap, dtype=jnp.int32)[:, None] == place[None, :]).astype(jnp.bfloat16)
    chosen = jnp.dot(
        pick, tiles.reshape(-1, 8 * 128), preferred_element_type=jnp.float32
    ).astype(jnp.bfloat16)
    deliver = chosen.reshape(n_far, cap * 8, 128)
    arrived = lax.all_to_all(deliver, "far", split_axis=0, concat_axis=0, tiled=True)

    owned = arrived.reshape(row_tiles, col_tiles, cap, 8, 128)
    owned = owned.transpose(2, 0, 3, 1, 4).reshape(cap, rows, width)
    gathered = broadcast_gather(owned, "dp").transpose(1, 0, 2, 3).reshape(cap, width, width)

    left_gram = jnp.einsum("crb,cnb->crn", owned, gathered, preferred_element_type=jnp.float32)
    my_columns = lax.dynamic_slice_in_dim(gathered, my_dp * rows, rows, 2)
    right_gram = jnp.einsum("cnr,cnb->crb", my_columns, gathered, preferred_element_type=jnp.float32)
    left_new = decay_rate * left_stat + (1.0 - decay_rate) * left_gram
    right_new = decay_rate * right_stat + (1.0 - decay_rate) * right_gram

    applied = jnp.einsum(
        "crn,cnb->crb", root, gathered, preferred_element_type=jnp.float32
    ).astype(jnp.bfloat16)
    factor = (right_eigen + epsilon) ** (-0.25)
    scaled = jnp.einsum("crb,cbe->cre", applied, right_basis, preferred_element_type=jnp.float32)
    scaled = (scaled * factor[:, None, :]).astype(jnp.bfloat16)
    update = jnp.einsum(
        "cre,cbe->crb", scaled, right_basis, preferred_element_type=jnp.float32
    ).astype(jnp.bfloat16)
    return (update, left_new, right_new)


def solution(mesh):
    n_dp, n_opt = mesh.devices.shape
    inner = Mesh(mesh.devices.reshape(n_dp, n_opt // NEAR, NEAR), ("dp", "far", "near"))
    opt = ("far", "near")
    in_specs = (
        P("dp", opt, None, None),
        P(),
        P(opt, "dp", None),
        P(opt, None, None),
        P(opt, None),
        P(opt, "dp", None),
        P(opt, "dp", None),
    )
    out_specs = (P(opt, None, None), P(opt, "dp", None), P(opt, "dp", None))
    return jax.shard_map(body, mesh=inner, in_specs=in_specs, out_specs=out_specs, check_vma=False)
```

```python
import jax
import jax.numpy as jnp
from jax import lax
from jax.experimental import pallas as pl
from jax.experimental.pallas import tpu as pltpu
from jax.sharding import Mesh, PartitionSpec as P

decay_rate = 0.9
epsilon = 1e-06
NEAR = 4


SIDE = 4
ALL = ("dp", "far", "near")


def broadcast_gather(x, axis, groups=None):
    n = lax.axis_size(axis) if groups is None else len(groups[0])
    copies = jnp.broadcast_to(x[None], (n,) + x.shape)
    return lax.all_to_all(
        copies, axis, split_axis=0, concat_axis=0, tiled=True, axis_index_groups=groups
    )


def side_groups(n_dp, n_opt, parity):
    groups = []
    for opt in range(n_opt):
        for fixed in range(SIDE):
            along_x = [(v * SIDE + fixed) * n_opt + opt for v in range(SIDE)]
            along_y = [(fixed * SIDE + v) * n_opt + opt for v in range(SIDE)]
            groups.append(along_x if opt % 2 == parity else along_y)
    return groups


def contract(a, b, dim_a, dim_b):
    return lax.dot_general(
        a, b, (((dim_a,), (dim_b,)), ((), ())), preferred_element_type=jnp.float32
    )


def slot_kernel(where, recv, root, basis, factor, left, right, update, left_new, right_new, g, gram):
    my_dp, core = where[0], where[1]
    rows = left.shape[1]
    for d in range(SIDE * SIDE):
        x, y = d // SIDE, d % SIDE
        first = jnp.where(core == 0, y, x)
        second = jnp.where(core == 0, x, y)
        g[d * rows : (d + 1) * rows, :] = recv[first, second, 0]
    block = g[...]
    applied = contract(root[0], block, 1, 0).astype(jnp.bfloat16)
    own = g[pl.ds(pl.multiple_of(my_dp * rows, rows), rows), :]
    left_new[0] = decay_rate * left[0] + (1.0 - decay_rate) * contract(own, block, 1, 1)
    group = 128 // rows
    lanes = pl.ds(pl.multiple_of(my_dp // group * 128, 128), 128)
    gram[...] = contract(g[:, lanes], block, 0, 0)
    mine = gram[pl.ds(pl.multiple_of(my_dp % group * rows, rows), rows), :]
    right_new[0] = decay_rate * right[0] + (1.0 - decay_rate) * mine
    scaled = (contract(applied, basis[0], 1, 0) * factor[0]).astype(jnp.bfloat16)
    update[0] = contract(scaled, basis[0], 1, 1).astype(jnp.bfloat16)


def slot_step(where, recv, root, basis, factor, left, right):
    cap, width, _ = basis.shape
    rows = left.shape[1]
    whole = pl.BlockSpec((1, width, width), lambda s, w: (s, 0, 0))
    slab = pl.BlockSpec((1, rows, width), lambda s, w: (s, 0, 0))
    return pl.pallas_call(
        slot_kernel,
        grid_spec=pltpu.PrefetchScalarGridSpec(
            num_scalar_prefetch=1,
            grid=(cap,),
            in_specs=[
                pl.BlockSpec((SIDE, SIDE, 1, rows, width), lambda s, w: (0, 0, s, 0, 0)),
                whole,
                whole,
                pl.BlockSpec((1, 1, width), lambda s, w: (s, 0, 0)),
                slab,
                slab,
            ],
            out_specs=[whole, slab, slab],
            scratch_shapes=[
                pltpu.VMEM((width, width), jnp.bfloat16),
                pltpu.VMEM((128, width), jnp.float32),
            ],
        ),
        out_shape=[
            jax.ShapeDtypeStruct(basis.shape, jnp.bfloat16),
            jax.ShapeDtypeStruct(left.shape, jnp.float32),
            jax.ShapeDtypeStruct(right.shape, jnp.float32),
        ],
        compiler_params=pltpu.CompilerParams(vmem_limit_bytes=32 * 1024 * 1024),
        cost_estimate=pl.CostEstimate(
            flops=7 * cap * width**3, bytes_accessed=10 * cap * width**2, transcendentals=0
        ),
    )(where, recv, root, basis, factor, left, right)


def body(gradients, owner_map, left_root, right_basis, right_eigen, left_stat, right_stat):
    n_dp, n_far, n_near = lax.axis_size("dp"), lax.axis_size("far"), lax.axis_size("near")
    _, blocks, width, _ = gradients.shape
    cap, rows, _ = left_stat.shape
    my_dp, my_near = lax.axis_index("dp"), lax.axis_index("near")
    row_tiles, col_tiles = rows // 8, width // 128

    root = lax.all_gather(left_root, "dp", axis=1, tiled=True)

    sent = gradients.reshape(blocks, n_dp, row_tiles, 8, col_tiles, 128)
    sent = sent.transpose(1, 2, 4, 0, 3, 5).reshape(n_dp, n_far, blocks * 8, 128)
    parts = lax.all_to_all(sent, "dp", split_axis=0, concat_axis=0, tiled=True)
    summed = jnp.sum(parts.astype(jnp.float32), axis=0).astype(jnp.bfloat16)

    spread = lax.all_to_all(summed, "far", split_axis=0, concat_axis=0, tiled=True)
    tiles = broadcast_gather(spread, "near")
    tiles = tiles.reshape(n_near, n_far, blocks, 8, 128)

    owners = owner_map
    same = owners[:, None] == owners[None, :]
    order = jnp.arange(owners.shape[0], dtype=jnp.int32)
    slot = jnp.sum((same & (order[None, :] < order[:, None])).astype(jnp.int32), axis=1)
    place = jnp.where(owners % n_near == my_near, owners // n_near * cap + slot, -1)
    place = place.reshape(n_far, n_near, blocks).transpose(1, 0, 2).reshape(-1)
    pick = (jnp.arange(n_far * cap, dtype=jnp.int32)[:, None] == place[None, :]).astype(jnp.bfloat16)
    chosen = jnp.dot(
        pick, tiles.reshape(-1, 8 * 128), preferred_element_type=jnp.float32
    ).astype(jnp.bfloat16)
    deliver = chosen.reshape(n_far, cap * 8, 128)
    arrived = lax.all_to_all(deliver, "far", split_axis=0, concat_axis=0, tiled=True)

    owned = arrived.reshape(row_tiles, col_tiles, cap, 8, 128)
    owned = owned.transpose(2, 0, 3, 1, 4).reshape(cap, rows, width)
    n_opt = n_far * n_near
    line = broadcast_gather(owned, ALL, side_groups(n_dp, n_opt, 0))
    line, root = lax.optimization_barrier((line, root))
    recv = broadcast_gather(line, ALL, side_groups(n_dp, n_opt, 1))
    recv = recv.reshape(SIDE, SIDE, cap, rows, width)

    factor = (right_eigen + epsilon) ** (-0.25)
    where = jnp.stack([my_dp, my_near % 2]).astype(jnp.int32)
    update, left_new, right_new = slot_step(
        where, recv, root, right_basis, factor[:, None, :], left_stat, right_stat
    )
    return (update, left_new, right_new)


def solution(mesh):
    n_dp, n_opt = mesh.devices.shape
    inner = Mesh(mesh.devices.reshape(n_dp, n_opt // NEAR, NEAR), ("dp", "far", "near"))
    opt = ("far", "near")
    in_specs = (
        P("dp", opt, None, None),
        P(),
        P(opt, "dp", None),
        P(opt, None, None),
        P(opt, None),
        P(opt, "dp", None),
        P(opt, "dp", None),
    )
    out_specs = (P(opt, None, None), P(opt, "dp", None), P(opt, "dp", None))
    return jax.shard_map(body, mesh=inner, in_specs=in_specs, out_specs=out_specs, check_vma=False)
```

```python
import jax
import jax.numpy as jnp
from jax import lax
from jax.experimental import pallas as pl
from jax.experimental.pallas import tpu as pltpu
from jax.sharding import Mesh, PartitionSpec as P

decay_rate = 0.9
epsilon = 1e-06
CORES = 2
SIDE = 4
ALL = ("dp", "z", "core")
EVEN = ((0, 1), (2, 3))
ODD = ((1, 2), (0, 3))


def broadcast_gather(x, axis, groups=None):
    n = lax.axis_size(axis) if groups is None else len(groups[0])
    copies = jnp.broadcast_to(x[None], (n,) + x.shape)
    return lax.all_to_all(
        copies, axis, split_axis=0, concat_axis=0, tiled=True, axis_index_groups=groups
    )


def quads(n_opt, parity):
    groups = []
    for opt in range(n_opt):
        pairs = EVEN if opt % CORES == parity else ODD
        for across in pairs:
            for along in pairs:
                groups.append([(x * SIDE + y) * n_opt + opt for x in across for y in along])
    return groups


def contract(a, b, dim_a, dim_b):
    return lax.dot_general(
        a, b, (((dim_a,), (dim_b,)), ((), ())), preferred_element_type=jnp.float32
    )


def slot_kernel(where, recv, root, basis, factor, left, right, update, left_new, right_new, g, gram):
    my_dp, core = where[0], where[1]
    rows = left.shape[1]
    flip_x = my_dp // SIDE // 2 == 0
    flip_y = my_dp % SIDE // 2 == 0
    for d in range(SIDE * SIDE):
        x, y = d // SIDE, d % SIDE
        outer_x, outer_y = int(x in (0, 3)), int(y in (0, 3))
        odd_x = jnp.where(flip_x, 1 - outer_x, outer_x)
        odd_y = jnp.where(flip_y, 1 - outer_y, outer_y)
        high = x // 2 * 2 + y // 2
        first = jnp.where(core == 0, high, odd_x * 2 + odd_y)
        second = jnp.where(core == 0, x % 2 * 2 + y % 2, high)
        g[d * rows : (d + 1) * rows, :] = recv[first, second, 0]
    block = g[...]
    applied = contract(root[0], block, 1, 0).astype(jnp.bfloat16)
    own = g[pl.ds(pl.multiple_of(my_dp * rows, rows), rows), :]
    left_new[0] = decay_rate * left[0] + (1.0 - decay_rate) * contract(own, block, 1, 1)
    group = 128 // rows
    lanes = pl.ds(pl.multiple_of(my_dp // group * 128, 128), 128)
    gram[...] = contract(g[:, lanes], block, 0, 0)
    mine = gram[pl.ds(pl.multiple_of(my_dp % group * rows, rows), rows), :]
    right_new[0] = decay_rate * right[0] + (1.0 - decay_rate) * mine
    scaled = (contract(applied, basis[0], 1, 0) * factor[0]).astype(jnp.bfloat16)
    update[0] = contract(scaled, basis[0], 1, 1).astype(jnp.bfloat16)


def slot_step(where, recv, root, basis, factor, left, right):
    cap, width, _ = basis.shape
    rows = left.shape[1]
    whole = pl.BlockSpec((1, width, width), lambda s, w: (s, 0, 0))
    slab = pl.BlockSpec((1, rows, width), lambda s, w: (s, 0, 0))
    return pl.pallas_call(
        slot_kernel,
        grid_spec=pltpu.PrefetchScalarGridSpec(
            num_scalar_prefetch=1,
            grid=(cap,),
            in_specs=[
                pl.BlockSpec((4, 4, 1, rows, width), lambda s, w: (0, 0, s, 0, 0)),
                whole,
                whole,
                pl.BlockSpec((1, 1, width), lambda s, w: (s, 0, 0)),
                slab,
                slab,
            ],
            out_specs=[whole, slab, slab],
            scratch_shapes=[
                pltpu.VMEM((width, width), jnp.bfloat16),
                pltpu.VMEM((128, width), jnp.float32),
            ],
        ),
        out_shape=[
            jax.ShapeDtypeStruct(basis.shape, jnp.bfloat16),
            jax.ShapeDtypeStruct(left.shape, jnp.float32),
            jax.ShapeDtypeStruct(right.shape, jnp.float32),
        ],
        compiler_params=pltpu.CompilerParams(vmem_limit_bytes=56 * 1024 * 1024),
        cost_estimate=pl.CostEstimate(
            flops=7 * cap * width**3, bytes_accessed=10 * cap * width**2, transcendentals=0
        ),
    )(where, recv, root, basis, factor, left, right)


def body(gradients, owner_map, left_root, right_basis, right_eigen, left_stat, right_stat):
    n_dp, n_z = lax.axis_size("dp"), lax.axis_size("z")
    _, blocks, width, _ = gradients.shape
    cap, rows, _ = left_stat.shape
    my_dp, my_core = lax.axis_index("dp"), lax.axis_index("core")
    row_tiles, col_tiles = rows // 8, width // 128

    root = lax.all_gather(left_root, "dp", axis=1, tiled=True)

    sent = gradients.reshape(blocks, n_dp, rows, width).transpose(1, 0, 2, 3)
    parts = lax.all_to_all(sent, "dp", split_axis=0, concat_axis=0, tiled=True)
    summed = jnp.sum(parts.astype(jnp.float32), axis=0).astype(jnp.bfloat16)

    summed = summed.reshape(blocks, row_tiles, 2, 4, col_tiles, 128)
    pieces = summed.transpose(1, 4, 2, 0, 3, 5).reshape(n_z, blocks * 4, 128)
    spread = lax.all_to_all(pieces, "z", split_axis=0, concat_axis=0, tiled=True)
    swapped = lax.ppermute(spread, "core", [(0, 1), (1, 0)])
    held = jnp.concatenate([t.reshape(n_z * blocks, 4 * 128) for t in (spread, swapped)])

    same = owner_map[:, None] == owner_map[None, :]
    order = jnp.arange(owner_map.shape[0], dtype=jnp.int32)
    slot = jnp.sum((same & (order[None, :] < order[:, None])).astype(jnp.int32), axis=1)
    place = jnp.where(owner_map % CORES == my_core, owner_map // CORES * cap + slot, -1)
    place = place.reshape(n_z, CORES, blocks)
    first, second = place[:, 0].reshape(-1), place[:, 1].reshape(-1)
    place = jnp.concatenate(
        [jnp.where(my_core == 0, first, second), jnp.where(my_core == 0, second, first)]
    )
    pick = (jnp.arange(n_z * cap, dtype=jnp.int32)[:, None] == place[None, :]).astype(jnp.bfloat16)
    chosen = jnp.dot(pick, held, preferred_element_type=jnp.float32).astype(jnp.bfloat16)
    deliver = chosen.reshape(n_z, cap, 4, 128)
    arrived = lax.all_to_all(deliver, "z", split_axis=0, concat_axis=0, tiled=True)

    owned = arrived.reshape(row_tiles, col_tiles, 2, cap, 4, 128)
    owned = owned.transpose(3, 0, 2, 4, 1, 5).reshape(cap, rows, width)
    n_opt = n_z * CORES
    factor = (right_eigen + epsilon) ** (-0.25)
    where = jnp.stack([my_dp, my_core]).astype(jnp.int32)
    line = broadcast_gather(owned, ALL, quads(n_opt, 0))
    line, root, factor, where = lax.optimization_barrier((line, root, factor, where))
    recv = broadcast_gather(line, ALL, quads(n_opt, 1))

    update, left_new, right_new = slot_step(
        where, recv, root, right_basis, factor[:, None, :], left_stat, right_stat
    )
    return (update, left_new, right_new)


def solution(mesh):
    n_dp, n_opt = mesh.devices.shape
    inner = Mesh(mesh.devices.reshape(n_dp, n_opt // CORES, CORES), ALL)
    opt = ("z", "core")
    in_specs = (
        P("dp", opt, None, None),
        P(),
        P(opt, "dp", None),
        P(opt, None, None),
        P(opt, None),
        P(opt, "dp", None),
        P(opt, "dp", None),
    )
    out_specs = (P(opt, None, None), P(opt, "dp", None), P(opt, "dp", None))
    return jax.shard_map(body, mesh=inner, in_specs=in_specs, out_specs=out_specs, check_vma=False)
```

```python
import jax
import jax.numpy as jnp
from jax import lax
from jax.experimental import pallas as pl
from jax.experimental.pallas import tpu as pltpu
from jax.sharding import Mesh, PartitionSpec as P

decay_rate = 0.9
epsilon = 1e-06
CORES = 2
SIDE = 4
ALL = ("dp", "z", "core")
EVEN = ((0, 1), (2, 3))
ODD = ((1, 2), (0, 3))


def broadcast_gather(x, axis, groups=None):
    n = lax.axis_size(axis) if groups is None else len(groups[0])
    copies = jnp.broadcast_to(x[None], (n,) + x.shape)
    return lax.all_to_all(
        copies, axis, split_axis=0, concat_axis=0, tiled=True, axis_index_groups=groups
    )


def quads(n_opt):
    groups = []
    for opt in range(n_opt):
        pairs = EVEN if opt % CORES == 0 else ODD
        for across in pairs:
            for along in pairs:
                groups.append([(x * SIDE + y) * n_opt + opt for x in across for y in along])
    return groups


def swap_corner(x, across, along):
    def partner(v, core, moved):
        return v if not moved else (SIDE - 1 - v if core == 0 else v ^ 1)

    n_opt = lax.axis_size("z") * CORES
    pairs = []
    for source in range(SIDE * SIDE * n_opt):
        d, opt = divmod(source, n_opt)
        px = partner(d // SIDE, opt % CORES, across)
        py = partner(d % SIDE, opt % CORES, along)
        pairs.append((source, (px * SIDE + py) * n_opt + opt))
    return lax.ppermute(x, ALL, pairs)


def contract(a, b, dim_a, dim_b):
    return lax.dot_general(
        a, b, (((dim_a,), (dim_b,)), ((), ())), preferred_element_type=jnp.float32
    )


def slot_kernel(where, own4, along4, across4, corner4, root, basis, factor, left, right, update, left_new, right_new, g, gram):
    my_dp, core = where[0], where[1]
    rows = left.shape[1]
    my_x, my_y = my_dp // SIDE, my_dp % SIDE

    def spot(mine, moved, member):
        half = jnp.where(mine >= 2, 1, 0)
        outer = jnp.where((mine == 0) | (mine == SIDE - 1), 1, 0)
        if moved:
            half, outer = 1 - half, 1 - outer
        return jnp.where(core == 0, half * 2 + member, 2 + outer if member else 1 - outer)

    for step, rows4 in enumerate((own4, along4, across4, corner4)):
        for member in range(SIDE):
            x = spot(my_x, step // 2, member // 2)
            y = spot(my_y, step % 2, member % 2)
            first = pl.multiple_of((x * SIDE + y) * rows, rows)
            g[pl.ds(first, rows), :] = rows4[member, 0]
    block = g[...]
    applied = contract(root[0], block, 1, 0).astype(jnp.bfloat16)
    own = g[pl.ds(pl.multiple_of(my_dp * rows, rows), rows), :]
    left_new[0] = decay_rate * left[0] + (1.0 - decay_rate) * contract(own, block, 1, 1)
    group = 128 // rows
    lanes = pl.ds(pl.multiple_of(my_dp // group * 128, 128), 128)
    gram[...] = contract(g[:, lanes], block, 0, 0)
    mine = gram[pl.ds(pl.multiple_of(my_dp % group * rows, rows), rows), :]
    right_new[0] = decay_rate * right[0] + (1.0 - decay_rate) * mine
    scaled = (contract(applied, basis[0], 1, 0) * factor[0]).astype(jnp.bfloat16)
    update[0] = contract(scaled, basis[0], 1, 1).astype(jnp.bfloat16)


def slot_step(where, squares, root, basis, factor, left, right):
    cap, width, _ = basis.shape
    rows = left.shape[1]
    square = pl.BlockSpec((SIDE, 1, rows, width), lambda s, w: (0, s, 0, 0))
    whole = pl.BlockSpec((1, width, width), lambda s, w: (s, 0, 0))
    slab = pl.BlockSpec((1, rows, width), lambda s, w: (s, 0, 0))
    return pl.pallas_call(
        slot_kernel,
        grid_spec=pltpu.PrefetchScalarGridSpec(
            num_scalar_prefetch=1,
            grid=(cap,),
            in_specs=[
                square,
                square,
                square,
                square,
                whole,
                whole,
                pl.BlockSpec((1, 1, width), lambda s, w: (s, 0, 0)),
                slab,
                slab,
            ],
            out_specs=[whole, slab, slab],
            scratch_shapes=[
                pltpu.VMEM((width, width), jnp.bfloat16),
                pltpu.VMEM((128, width), jnp.float32),
            ],
        ),
        out_shape=[
            jax.ShapeDtypeStruct(basis.shape, jnp.bfloat16),
            jax.ShapeDtypeStruct(left.shape, jnp.float32),
            jax.ShapeDtypeStruct(right.shape, jnp.float32),
        ],
        compiler_params=pltpu.CompilerParams(vmem_limit_bytes=48 * 1024 * 1024),
        cost_estimate=pl.CostEstimate(
            flops=7 * cap * width**3, bytes_accessed=10 * cap * width**2, transcendentals=0
        ),
    )(where, *squares, root, basis, factor, left, right)


def body(gradients, owner_map, left_root, right_basis, right_eigen, left_stat, right_stat):
    n_dp, n_z = lax.axis_size("dp"), lax.axis_size("z")
    _, blocks, width, _ = gradients.shape
    cap, rows, _ = left_stat.shape
    my_dp, my_core = lax.axis_index("dp"), lax.axis_index("core")
    row_tiles, col_tiles = rows // 8, width // 128

    root = lax.all_gather(left_root, "dp", axis=1, tiled=True)

    sent = gradients.reshape(blocks, n_dp, rows, width).transpose(1, 0, 2, 3)
    parts = lax.all_to_all(sent, "dp", split_axis=0, concat_axis=0, tiled=True)
    summed = jnp.sum(parts.astype(jnp.float32), axis=0).astype(jnp.bfloat16)

    summed = summed.reshape(blocks, row_tiles, 2, 4, col_tiles, 128)
    pieces = summed.transpose(1, 4, 2, 0, 3, 5).reshape(n_z, blocks * 4, 128)
    spread = lax.all_to_all(pieces, "z", split_axis=0, concat_axis=0, tiled=True)
    swapped = lax.ppermute(spread, "core", [(0, 1), (1, 0)])
    held = jnp.concatenate([t.reshape(n_z * blocks, 4 * 128) for t in (spread, swapped)])

    same = owner_map[:, None] == owner_map[None, :]
    order = jnp.arange(owner_map.shape[0], dtype=jnp.int32)
    slot = jnp.sum((same & (order[None, :] < order[:, None])).astype(jnp.int32), axis=1)
    place = jnp.where(owner_map % CORES == my_core, owner_map // CORES * cap + slot, -1)
    place = place.reshape(n_z, CORES, blocks)
    first, second = place[:, 0].reshape(-1), place[:, 1].reshape(-1)
    place = jnp.concatenate(
        [jnp.where(my_core == 0, first, second), jnp.where(my_core == 0, second, first)]
    )
    pick = (jnp.arange(n_z * cap, dtype=jnp.int32)[:, None] == place[None, :]).astype(jnp.bfloat16)
    chosen = jnp.dot(pick, held, preferred_element_type=jnp.float32).astype(jnp.bfloat16)
    deliver = chosen.reshape(n_z, cap, 4, 128)
    arrived = lax.all_to_all(deliver, "z", split_axis=0, concat_axis=0, tiled=True)

    owned = arrived.reshape(row_tiles, col_tiles, 2, cap, 4, 128)
    owned = owned.transpose(3, 0, 2, 4, 1, 5).reshape(cap, rows, width)
    n_opt = n_z * CORES
    factor = (right_eigen + epsilon) ** (-0.25)
    where = jnp.stack([my_dp, my_core]).astype(jnp.int32)
    line = broadcast_gather(owned, ALL, quads(n_opt))
    line, root, factor, where = lax.optimization_barrier((line, root, factor, where))
    squares = [line] + [swap_corner(line, a, b) for a, b in ((False, True), (True, False), (True, True))]

    update, left_new, right_new = slot_step(
        where, squares, root, right_basis, factor[:, None, :], left_stat, right_stat
    )
    return (update, left_new, right_new)


def solution(mesh):
    n_dp, n_opt = mesh.devices.shape
    inner = Mesh(mesh.devices.reshape(n_dp, n_opt // CORES, CORES), ALL)
    opt = ("z", "core")
    in_specs = (
        P("dp", opt, None, None),
        P(),
        P(opt, "dp", None),
        P(opt, None, None),
        P(opt, None),
        P(opt, "dp", None),
        P(opt, "dp", None),
    )
    out_specs = (P(opt, None, None), P(opt, "dp", None), P(opt, "dp", None))
    return jax.shard_map(body, mesh=inner, in_specs=in_specs, out_specs=out_specs, check_vma=False)
```

```python
import jax
import jax.numpy as jnp
from jax import lax
from jax.experimental import pallas as pl
from jax.experimental.pallas import tpu as pltpu
from jax.sharding import Mesh, PartitionSpec as P

decay_rate = 0.9
epsilon = 1e-06
CORES = 2
SIDE = 4
ALL = ("dp", "z", "core")
EVEN = ((0, 1), (2, 3))
ODD = ((1, 2), (0, 3))


def broadcast_gather(x, axis, groups=None):
    n = lax.axis_size(axis) if groups is None else len(groups[0])
    copies = jnp.broadcast_to(x[None], (n,) + x.shape)
    return lax.all_to_all(
        copies, axis, split_axis=0, concat_axis=0, tiled=True, axis_index_groups=groups
    )


def quads(n_opt):
    groups = []
    for opt in range(n_opt):
        pairs = EVEN if opt % CORES == 0 else ODD
        for across in pairs:
            for along in pairs:
                groups.append([(x * SIDE + y) * n_opt + opt for x in across for y in along])
    return groups


def swap_corner(x, across, along):
    def partner(v, core, moved):
        return v if not moved else (SIDE - 1 - v if core == 0 else v ^ 1)

    n_opt = lax.axis_size("z") * CORES
    pairs = []
    for source in range(SIDE * SIDE * n_opt):
        d, opt = divmod(source, n_opt)
        px = partner(d // SIDE, opt % CORES, across)
        py = partner(d % SIDE, opt % CORES, along)
        pairs.append((source, (px * SIDE + py) * n_opt + opt))
    return lax.ppermute(x, ALL, pairs)


def contract(a, b, dim_a, dim_b):
    return lax.dot_general(
        a, b, (((dim_a,), (dim_b,)), ((), ())), preferred_element_type=jnp.float32
    )


def slot_kernel(where, own4, along4, across4, corner4, root, middle, left, right, update, left_new, right_new, g, gram):
    my_dp, core = where[0], where[1]
    rows = left.shape[1]
    my_x, my_y = my_dp // SIDE, my_dp % SIDE

    def spot(mine, moved, member):
        half = jnp.where(mine >= 2, 1, 0)
        outer = jnp.where((mine == 0) | (mine == SIDE - 1), 1, 0)
        if moved:
            half, outer = 1 - half, 1 - outer
        return jnp.where(core == 0, half * 2 + member, 2 + outer if member else 1 - outer)

    for step, rows4 in enumerate((own4, along4, across4, corner4)):
        for member in range(SIDE):
            x = spot(my_x, step // 2, member // 2)
            y = spot(my_y, step % 2, member % 2)
            first = pl.multiple_of((x * SIDE + y) * rows, rows)
            g[pl.ds(first, rows), :] = rows4[member, 0]
    block = g[...]
    applied = contract(root[0], block, 1, 0).astype(jnp.bfloat16)
    own = g[pl.ds(pl.multiple_of(my_dp * rows, rows), rows), :]
    left_new[0] = decay_rate * left[0] + (1.0 - decay_rate) * contract(own, block, 1, 1)
    group = 128 // rows
    lanes = pl.ds(pl.multiple_of(my_dp // group * 128, 128), 128)
    gram[...] = contract(g[:, lanes], block, 0, 0)
    mine = gram[pl.ds(pl.multiple_of(my_dp % group * rows, rows), rows), :]
    right_new[0] = decay_rate * right[0] + (1.0 - decay_rate) * mine
    update[0] = contract(applied, middle[0], 1, 0).astype(jnp.bfloat16)


def middle_kernel(basis, factor, middle):
    scaled = basis[0].astype(jnp.float32) * factor[0]
    high = scaled.astype(jnp.bfloat16)
    low = (scaled - high.astype(jnp.float32)).astype(jnp.bfloat16)
    product = contract(high, basis[0], 1, 1) + contract(low, basis[0], 1, 1)
    middle[0] = product.astype(jnp.bfloat16)


def middle_step(basis, factor):
    cap, width, _ = basis.shape
    whole = pl.BlockSpec((1, width, width), lambda s: (s, 0, 0))
    return pl.pallas_call(
        middle_kernel,
        grid=(cap,),
        in_specs=[whole, pl.BlockSpec((1, 1, width), lambda s: (s, 0, 0))],
        out_specs=whole,
        out_shape=jax.ShapeDtypeStruct(basis.shape, jnp.bfloat16),
        compiler_params=pltpu.CompilerParams(vmem_limit_bytes=58 * 1024 * 1024),
        cost_estimate=pl.CostEstimate(
            flops=4 * cap * width**3, bytes_accessed=4 * cap * width**2, transcendentals=0
        ),
    )(basis, factor)


def slot_step(where, squares, root, middle, left, right):
    cap, width, _ = middle.shape
    rows = left.shape[1]
    square = pl.BlockSpec((SIDE, 1, rows, width), lambda s, w: (0, s, 0, 0))
    whole = pl.BlockSpec((1, width, width), lambda s, w: (s, 0, 0))
    slab = pl.BlockSpec((1, rows, width), lambda s, w: (s, 0, 0))
    return pl.pallas_call(
        slot_kernel,
        grid_spec=pltpu.PrefetchScalarGridSpec(
            num_scalar_prefetch=1,
            grid=(cap,),
            in_specs=[
                square,
                square,
                square,
                square,
                whole,
                whole,
                slab,
                slab,
            ],
            out_specs=[whole, slab, slab],
            scratch_shapes=[
                pltpu.VMEM((width, width), jnp.bfloat16),
                pltpu.VMEM((128, width), jnp.float32),
            ],
        ),
        out_shape=[
            jax.ShapeDtypeStruct(middle.shape, jnp.bfloat16),
            jax.ShapeDtypeStruct(left.shape, jnp.float32),
            jax.ShapeDtypeStruct(right.shape, jnp.float32),
        ],
        compiler_params=pltpu.CompilerParams(vmem_limit_bytes=58 * 1024 * 1024),
        cost_estimate=pl.CostEstimate(
            flops=5 * cap * width**3, bytes_accessed=10 * cap * width**2, transcendentals=0
        ),
    )(where, *squares, root, middle, left, right)


def body(gradients, owner_map, left_root, right_basis, right_eigen, left_stat, right_stat):
    n_dp, n_z = lax.axis_size("dp"), lax.axis_size("z")
    _, blocks, width, _ = gradients.shape
    cap, rows, _ = left_stat.shape
    my_dp, my_core = lax.axis_index("dp"), lax.axis_index("core")
    row_tiles, col_tiles = rows // 8, width // 128

    root = lax.all_gather(left_root, "dp", axis=1, tiled=True)

    sent = gradients.reshape(blocks, n_dp, rows, width).transpose(1, 0, 2, 3)
    parts = lax.all_to_all(sent, "dp", split_axis=0, concat_axis=0, tiled=True)
    summed = jnp.sum(parts.astype(jnp.float32), axis=0).astype(jnp.bfloat16)

    summed = summed.reshape(blocks, row_tiles, 2, 4, col_tiles, 128)
    pieces = summed.transpose(1, 4, 2, 0, 3, 5).reshape(n_z, blocks * 4, 128)
    pieces, right_basis = lax.optimization_barrier((pieces, right_basis))
    factor = (right_eigen + epsilon) ** (-0.25)
    middle = middle_step(right_basis, factor[:, None, :])
    spread = lax.all_to_all(pieces, "z", split_axis=0, concat_axis=0, tiled=True)
    spread, middle = lax.optimization_barrier((spread, middle))
    swapped = lax.ppermute(spread, "core", [(0, 1), (1, 0)])
    held = jnp.concatenate([t.reshape(n_z * blocks, 4 * 128) for t in (spread, swapped)])

    same = owner_map[:, None] == owner_map[None, :]
    order = jnp.arange(owner_map.shape[0], dtype=jnp.int32)
    slot = jnp.sum((same & (order[None, :] < order[:, None])).astype(jnp.int32), axis=1)
    place = jnp.where(owner_map % CORES == my_core, owner_map // CORES * cap + slot, -1)
    place = place.reshape(n_z, CORES, blocks)
    first, second = place[:, 0].reshape(-1), place[:, 1].reshape(-1)
    place = jnp.concatenate(
        [jnp.where(my_core == 0, first, second), jnp.where(my_core == 0, second, first)]
    )
    pick = (jnp.arange(n_z * cap, dtype=jnp.int32)[:, None] == place[None, :]).astype(jnp.bfloat16)
    chosen = jnp.dot(pick, held, preferred_element_type=jnp.float32).astype(jnp.bfloat16)
    deliver = chosen.reshape(n_z, cap, 4, 128)
    arrived = lax.all_to_all(deliver, "z", split_axis=0, concat_axis=0, tiled=True)

    owned = arrived.reshape(row_tiles, col_tiles, 2, cap, 4, 128)
    owned = owned.transpose(3, 0, 2, 4, 1, 5).reshape(cap, rows, width)
    n_opt = n_z * CORES
    where = jnp.stack([my_dp, my_core]).astype(jnp.int32)
    line = broadcast_gather(owned, ALL, quads(n_opt))
    line, root, where = lax.optimization_barrier((line, root, where))
    squares = [line] + [swap_corner(line, a, b) for a, b in ((False, True), (True, False), (True, True))]

    update, left_new, right_new = slot_step(
        where, squares, root, middle, left_stat, right_stat
    )
    return (update, left_new, right_new)


def solution(mesh):
    n_dp, n_opt = mesh.devices.shape
    inner = Mesh(mesh.devices.reshape(n_dp, n_opt // CORES, CORES), ALL)
    opt = ("z", "core")
    in_specs = (
        P("dp", opt, None, None),
        P(),
        P(opt, "dp", None),
        P(opt, None, None),
        P(opt, None),
        P(opt, "dp", None),
        P(opt, "dp", None),
    )
    out_specs = (P(opt, None, None), P(opt, "dp", None), P(opt, "dp", None))
    return jax.shard_map(body, mesh=inner, in_specs=in_specs, out_specs=out_specs, check_vma=False)
```

```python
import jax
import jax.numpy as jnp
from jax import lax
from jax.experimental import pallas as pl
from jax.experimental.pallas import tpu as pltpu
from jax.sharding import Mesh, PartitionSpec as P

decay_rate = 0.9
epsilon = 1e-06
CORES = 2
SIDE = 4
ALL = ("dp", "z", "core")
EVEN = ((0, 1), (2, 3))
ODD = ((1, 2), (0, 3))


def broadcast_gather(x, axis, groups=None):
    n = lax.axis_size(axis) if groups is None else len(groups[0])
    copies = jnp.broadcast_to(x[None], (n,) + x.shape)
    return lax.all_to_all(
        copies, axis, split_axis=0, concat_axis=0, tiled=True, axis_index_groups=groups
    )


def quads(n_opt):
    groups = []
    for opt in range(n_opt):
        pairs = EVEN if opt % CORES == 0 else ODD
        for across in pairs:
            for along in pairs:
                groups.append([(x * SIDE + y) * n_opt + opt for x in across for y in along])
    return groups


def swap_corner(x, across, along):
    def partner(v, core, moved):
        return v if not moved else (SIDE - 1 - v if core == 0 else v ^ 1)

    n_opt = lax.axis_size("z") * CORES
    pairs = []
    for source in range(SIDE * SIDE * n_opt):
        d, opt = divmod(source, n_opt)
        px = partner(d // SIDE, opt % CORES, across)
        py = partner(d % SIDE, opt % CORES, along)
        pairs.append((source, (px * SIDE + py) * n_opt + opt))
    return lax.ppermute(x, ALL, pairs)


def contract(a, b, dim_a, dim_b):
    return lax.dot_general(
        a, b, (((dim_a,), (dim_b,)), ((), ())), preferred_element_type=jnp.float32
    )


def slot_kernel(
    where, own4, along4, across4, corner4, root, middle, left, right,
    update, left_new, right_new,
    g, gram, update_out, left_out, right_out, update_sem, left_sem, right_sem
):
    my_dp, core = where[0], where[1]
    cap, rows, _ = left.shape
    my_x, my_y = my_dp // SIDE, my_dp % SIDE

    def spot(mine, moved, member):
        half = jnp.where(mine >= 2, 1, 0)
        outer = jnp.where((mine == 0) | (mine == SIDE - 1), 1, 0)
        if moved:
            half, outer = 1 - half, 1 - outer
        return jnp.where(core == 0, half * 2 + member, 2 + outer if member else 1 - outer)

    spots = {
        (step, member): pl.multiple_of(
            (spot(my_x, step // 2, member // 2) * SIDE + spot(my_y, step % 2, member % 2)) * rows,
            rows,
        )
        for step in range(SIDE)
        for member in range(SIDE)
    }
    group = 128 // rows
    own_rows = pl.ds(pl.multiple_of(my_dp * rows, rows), rows)
    lanes = pl.ds(pl.multiple_of(my_dp // group * 128, 128), 128)
    gram_rows = pl.ds(pl.multiple_of(my_dp % group * rows, rows), rows)
    results = []

    def send(source, target, sem, s):
        copy = pltpu.make_async_copy(source.at[s], target.at[s], sem.at[s])
        copy.start()
        results.append(copy)

    for s in range(cap):
        for step, rows4 in enumerate((own4, along4, across4, corner4)):
            for member in range(SIDE):
                g[s, pl.ds(spots[step, member], rows), :] = rows4[member, s]
        block = g[s]
        left_gram = contract(g[s, own_rows, :], block, 1, 1)
        left_out[s] = decay_rate * left[s] + (1.0 - decay_rate) * left_gram
        send(left_out, left_new, left_sem, s)
        gram[s] = contract(g[s, :, lanes], block, 0, 0)
        right_out[s] = decay_rate * right[s] + (1.0 - decay_rate) * gram[s, gram_rows, :]
        send(right_out, right_new, right_sem, s)
        applied = contract(root[s], block, 1, 0).astype(jnp.bfloat16)
        update_out[s] = contract(applied, middle[s], 1, 0).astype(jnp.bfloat16)
        send(update_out, update, update_sem, s)
    for copy in results:
        copy.wait()


def middle_kernel(basis, factor, middle):
    scaled = basis[0].astype(jnp.float32) * factor[0]
    high = scaled.astype(jnp.bfloat16)
    low = (scaled - high.astype(jnp.float32)).astype(jnp.bfloat16)
    product = contract(high, basis[0], 1, 1) + contract(low, basis[0], 1, 1)
    middle[0] = product.astype(jnp.bfloat16)


def middle_step(basis, factor):
    cap, width, _ = basis.shape
    whole = pl.BlockSpec((1, width, width), lambda s: (s, 0, 0))
    return pl.pallas_call(
        middle_kernel,
        grid=(cap,),
        in_specs=[whole, pl.BlockSpec((1, 1, width), lambda s: (s, 0, 0))],
        out_specs=whole,
        out_shape=jax.ShapeDtypeStruct(basis.shape, jnp.bfloat16),
        compiler_params=pltpu.CompilerParams(vmem_limit_bytes=58 * 1024 * 1024),
        cost_estimate=pl.CostEstimate(
            flops=4 * cap * width**3, bytes_accessed=4 * cap * width**2, transcendentals=0
        ),
    )(basis, factor)


def stage_kernel(source, target, sem):
    copy = pltpu.make_async_copy(source, target, sem)
    copy.start()
    copy.wait()


def stage(x):
    return pl.pallas_call(
        stage_kernel,
        in_specs=[pl.BlockSpec(memory_space=pl.ANY)],
        out_specs=pl.BlockSpec(memory_space=pltpu.VMEM),
        scratch_shapes=[pltpu.SemaphoreType.DMA],
        out_shape=jax.ShapeDtypeStruct(x.shape, x.dtype),
        compiler_params=pltpu.CompilerParams(vmem_limit_bytes=32 * 1024 * 1024),
        cost_estimate=pl.CostEstimate(flops=0, bytes_accessed=4 * x.size, transcendentals=0),
    )(x)


def slot_step(where, squares, root, middle, left, right):
    cap, width, _ = middle.shape
    rows = left.shape[1]
    near = pl.BlockSpec(memory_space=pltpu.VMEM)
    away = pl.BlockSpec(memory_space=pl.ANY)
    return pl.pallas_call(
        slot_kernel,
        in_specs=[pl.BlockSpec(memory_space=pltpu.SMEM)] + [near] * 8,
        out_specs=[away] * 3,
        scratch_shapes=[
            pltpu.VMEM((cap, width, width), jnp.bfloat16),
            pltpu.VMEM((cap, 128, width), jnp.float32),
            pltpu.VMEM((cap, width, width), jnp.bfloat16),
            pltpu.VMEM(left.shape, jnp.float32),
            pltpu.VMEM(right.shape, jnp.float32),
        ]
        + [pltpu.SemaphoreType.DMA((cap,))] * 3,
        out_shape=[
            jax.ShapeDtypeStruct(middle.shape, jnp.bfloat16),
            jax.ShapeDtypeStruct(left.shape, jnp.float32),
            jax.ShapeDtypeStruct(right.shape, jnp.float32),
        ],
        compiler_params=pltpu.CompilerParams(vmem_limit_bytes=32 * 1024 * 1024),
        cost_estimate=pl.CostEstimate(
            flops=5 * cap * width**3, bytes_accessed=10 * cap * width**2, transcendentals=0
        ),
    )(where, *squares, root, middle, left, right)


def body(gradients, owner_map, left_root, right_basis, right_eigen, left_stat, right_stat):
    n_dp, n_z = lax.axis_size("dp"), lax.axis_size("z")
    _, blocks, width, _ = gradients.shape
    cap, rows, _ = left_stat.shape
    my_dp, my_core = lax.axis_index("dp"), lax.axis_index("core")
    row_tiles, col_tiles = rows // 8, width // 128

    root = lax.all_gather(left_root, "dp", axis=1, tiled=True)

    sent = gradients.reshape(blocks, n_dp, rows, width).transpose(1, 0, 2, 3)
    parts = lax.all_to_all(sent, "dp", split_axis=0, concat_axis=0, tiled=True)
    summed = jnp.sum(parts.astype(jnp.float32), axis=0).astype(jnp.bfloat16)

    summed = summed.reshape(blocks, row_tiles, 2, 4, col_tiles, 128)
    pieces = summed.transpose(1, 4, 2, 0, 3, 5).reshape(n_z, blocks * 4, 128)
    pieces, right_basis, right_eigen, owner_map, my_dp, my_core = lax.optimization_barrier(
        (pieces, right_basis, right_eigen, owner_map, my_dp, my_core)
    )
    where = jnp.stack([my_dp, my_core]).astype(jnp.int32)
    factor = (right_eigen + epsilon) ** (-0.25)
    middle = middle_step(right_basis, factor[:, None, :])
    spread = lax.all_to_all(pieces, "z", split_axis=0, concat_axis=0, tiled=True)
    spread, middle, where = lax.optimization_barrier((spread, middle, where))
    swapped = lax.ppermute(spread, "core", [(0, 1), (1, 0)])
    held = jnp.concatenate([t.reshape(n_z * blocks, 4 * 128) for t in (spread, swapped)])

    same = owner_map[:, None] == owner_map[None, :]
    order = jnp.arange(owner_map.shape[0], dtype=jnp.int32)
    slot = jnp.sum((same & (order[None, :] < order[:, None])).astype(jnp.int32), axis=1)
    place = jnp.where(owner_map % CORES == my_core, owner_map // CORES * cap + slot, -1)
    place = place.reshape(n_z, CORES, blocks)
    first, second = place[:, 0].reshape(-1), place[:, 1].reshape(-1)
    place = jnp.concatenate(
        [jnp.where(my_core == 0, first, second), jnp.where(my_core == 0, second, first)]
    )
    pick = (jnp.arange(n_z * cap, dtype=jnp.int32)[:, None] == place[None, :]).astype(jnp.bfloat16)
    chosen = jnp.dot(pick, held, preferred_element_type=jnp.float32).astype(jnp.bfloat16)
    deliver = chosen.reshape(n_z, cap, 4, 128)
    arrived = lax.all_to_all(deliver, "z", split_axis=0, concat_axis=0, tiled=True)

    owned = arrived.reshape(row_tiles, col_tiles, 2, cap, 4, 128)
    owned = owned.transpose(3, 0, 2, 4, 1, 5).reshape(cap, rows, width)
    n_opt = n_z * CORES
    line = broadcast_gather(owned, ALL, quads(n_opt))
    line, root = lax.optimization_barrier((line, root))
    squares = [line] + [swap_corner(line, a, b) for a, b in ((False, True), (True, False), (True, True))]

    update, left_new, right_new = slot_step(
        where, squares, stage(root), middle, left_stat, right_stat
    )
    return (update, left_new, right_new)


def solution(mesh):
    n_dp, n_opt = mesh.devices.shape
    inner = Mesh(mesh.devices.reshape(n_dp, n_opt // CORES, CORES), ALL)
    opt = ("z", "core")
    in_specs = (
        P("dp", opt, None, None),
        P(),
        P(opt, "dp", None),
        P(opt, None, None),
        P(opt, None),
        P(opt, "dp", None),
        P(opt, "dp", None),
    )
    out_specs = (P(opt, None, None), P(opt, "dp", None), P(opt, "dp", None))
    return jax.shard_map(body, mesh=inner, in_specs=in_specs, out_specs=out_specs, check_vma=False)
```

```python
import jax
import jax.numpy as jnp
from jax import lax
from jax.experimental import pallas as pl
from jax.experimental.pallas import tpu as pltpu
from jax.sharding import Mesh, PartitionSpec as P

decay_rate = 0.9
epsilon = 1e-06
CORES = 2
SIDE = 4
ALL = ("dp", "z", "core")
EVEN = ((0, 1), (2, 3))
ODD = ((1, 2), (0, 3))


def broadcast_gather(x, axis, groups=None):
    n = lax.axis_size(axis) if groups is None else len(groups[0])
    copies = jnp.broadcast_to(x[None], (n,) + x.shape)
    return lax.all_to_all(
        copies, axis, split_axis=0, concat_axis=0, tiled=True, axis_index_groups=groups
    )


def quads(n_opt):
    groups = []
    for opt in range(n_opt):
        pairs = EVEN if opt % CORES == 0 else ODD
        for across in pairs:
            for along in pairs:
                groups.append([(x * SIDE + y) * n_opt + opt for x in across for y in along])
    return groups


def swap_corner(x, across, along):
    def partner(v, core, moved):
        return v if not moved else (SIDE - 1 - v if core == 0 else v ^ 1)

    n_opt = lax.axis_size("z") * CORES
    pairs = []
    for source in range(SIDE * SIDE * n_opt):
        d, opt = divmod(source, n_opt)
        px = partner(d // SIDE, opt % CORES, across)
        py = partner(d % SIDE, opt % CORES, along)
        pairs.append((source, (px * SIDE + py) * n_opt + opt))
    return lax.ppermute(x, ALL, pairs)


def contract(a, b, dim_a, dim_b):
    return lax.dot_general(
        a, b, (((dim_a,), (dim_b,)), ((), ())), preferred_element_type=jnp.float32
    )


def slot_kernel(
    where, own4, along4, across4, corner4, root, middle, left, right,
    update, left_new, right_new,
    g, gram, update_out, left_out, right_out, update_sem, left_sem, right_sem
):
    my_dp, core = where[0], where[1]
    cap, rows, _ = left.shape
    my_x, my_y = my_dp // SIDE, my_dp % SIDE

    def spot(mine, moved, member):
        half = jnp.where(mine >= 2, 1, 0)
        outer = jnp.where((mine == 0) | (mine == SIDE - 1), 1, 0)
        if moved:
            half, outer = 1 - half, 1 - outer
        return jnp.where(core == 0, half * 2 + member, 2 + outer if member else 1 - outer)

    spots = {
        (step, member): pl.multiple_of(
            (spot(my_x, step // 2, member // 2) * SIDE + spot(my_y, step % 2, member % 2)) * rows,
            rows,
        )
        for step in range(SIDE)
        for member in range(SIDE)
    }
    group = 128 // rows
    own_rows = pl.ds(pl.multiple_of(my_dp * rows, rows), rows)
    lanes = pl.ds(pl.multiple_of(my_dp // group * 128, 128), 128)
    gram_rows = pl.ds(pl.multiple_of(my_dp % group * rows, rows), rows)
    results = []

    def send(source, target, sem, s):
        copy = pltpu.make_async_copy(source.at[s], target.at[s], sem.at[s])
        copy.start()
        results.append(copy)

    for s in range(cap):
        for step, rows4 in enumerate((own4, along4, across4, corner4)):
            for member in range(SIDE):
                g[s, pl.ds(spots[step, member], rows), :] = rows4[member, s]
        block = g[s]
        left_gram = contract(g[s, own_rows, :], block, 1, 1)
        left_out[s] = decay_rate * left[s] + (1.0 - decay_rate) * left_gram
        send(left_out, left_new, left_sem, s)
        gram[s] = contract(g[s, :, lanes], block, 0, 0)
        right_out[s] = decay_rate * right[s] + (1.0 - decay_rate) * gram[s, gram_rows, :]
        send(right_out, right_new, right_sem, s)
        applied = contract(root[s], block, 1, 0).astype(jnp.bfloat16)
        update_out[s] = contract(applied, middle[s], 1, 0).astype(jnp.bfloat16)
        send(update_out, update, update_sem, s)
    for copy in results:
        copy.wait()


def middle_kernel(basis, factor, middle):
    scaled = basis[0].astype(jnp.float32) * factor[0]
    high = scaled.astype(jnp.bfloat16)
    low = (scaled - high.astype(jnp.float32)).astype(jnp.bfloat16)
    product = contract(high, basis[0], 1, 1) + contract(low, basis[0], 1, 1)
    middle[0] = product.astype(jnp.bfloat16)


def middle_step(basis, factor):
    cap, width, _ = basis.shape
    whole = pl.BlockSpec((1, width, width), lambda s: (s, 0, 0))
    return pl.pallas_call(
        middle_kernel,
        grid=(cap,),
        in_specs=[whole, pl.BlockSpec((1, 1, width), lambda s: (s, 0, 0))],
        out_specs=whole,
        out_shape=jax.ShapeDtypeStruct(basis.shape, jnp.bfloat16),
        compiler_params=pltpu.CompilerParams(vmem_limit_bytes=58 * 1024 * 1024),
        cost_estimate=pl.CostEstimate(
            flops=4 * cap * width**3, bytes_accessed=4 * cap * width**2, transcendentals=0
        ),
    )(basis, factor)


def stage_kernel(source, target, sem):
    copy = pltpu.make_async_copy(source, target, sem)
    copy.start()
    copy.wait()


def stage(x):
    return pl.pallas_call(
        stage_kernel,
        in_specs=[pl.BlockSpec(memory_space=pl.ANY)],
        out_specs=pl.BlockSpec(memory_space=pltpu.VMEM),
        scratch_shapes=[pltpu.SemaphoreType.DMA],
        out_shape=jax.ShapeDtypeStruct(x.shape, x.dtype),
        compiler_params=pltpu.CompilerParams(vmem_limit_bytes=32 * 1024 * 1024),
        cost_estimate=pl.CostEstimate(flops=0, bytes_accessed=4 * x.size, transcendentals=0),
    )(x)


def slot_step(where, squares, root, middle, left, right):
    cap, width, _ = middle.shape
    rows = left.shape[1]
    near = pl.BlockSpec(memory_space=pltpu.VMEM)
    away = pl.BlockSpec(memory_space=pl.ANY)
    return pl.pallas_call(
        slot_kernel,
        in_specs=[pl.BlockSpec(memory_space=pltpu.SMEM)] + [near] * 8,
        out_specs=[away] * 3,
        scratch_shapes=[
            pltpu.VMEM((cap, width, width), jnp.bfloat16),
            pltpu.VMEM((cap, 128, width), jnp.float32),
            pltpu.VMEM((cap, width, width), jnp.bfloat16),
            pltpu.VMEM(left.shape, jnp.float32),
            pltpu.VMEM(right.shape, jnp.float32),
        ]
        + [pltpu.SemaphoreType.DMA((cap,))] * 3,
        out_shape=[
            jax.ShapeDtypeStruct(middle.shape, jnp.bfloat16),
            jax.ShapeDtypeStruct(left.shape, jnp.float32),
            jax.ShapeDtypeStruct(right.shape, jnp.float32),
        ],
        compiler_params=pltpu.CompilerParams(vmem_limit_bytes=32 * 1024 * 1024),
        cost_estimate=pl.CostEstimate(
            flops=5 * cap * width**3, bytes_accessed=10 * cap * width**2, transcendentals=0
        ),
    )(where, *squares, root, middle, left, right)


def body(gradients, owner_map, left_root, right_basis, right_eigen, left_stat, right_stat):
    n_dp, n_z = lax.axis_size("dp"), lax.axis_size("z")
    _, blocks, width, _ = gradients.shape
    cap, rows, _ = left_stat.shape
    my_dp, my_core = lax.axis_index("dp"), lax.axis_index("core")
    row_tiles, col_tiles = rows // 8, width // 128

    root = lax.all_gather(left_root, "dp", axis=1, tiled=True)

    sent = gradients.reshape(blocks, n_dp, rows, width).transpose(1, 0, 2, 3)
    sent, my_dp, my_core = lax.optimization_barrier((sent, my_dp, my_core))
    parts = lax.all_to_all(sent, "dp", split_axis=0, concat_axis=0, tiled=True)
    summed = jnp.sum(parts.astype(jnp.float32), axis=0).astype(jnp.bfloat16)

    summed = summed.reshape(blocks, row_tiles, 2, 4, col_tiles, 128)
    pieces = summed.transpose(1, 4, 2, 0, 3, 5).reshape(n_z, blocks * 4, 128)
    pieces, right_eigen, owner_map, my_dp, my_core = lax.optimization_barrier(
        (pieces, right_eigen, owner_map, my_dp, my_core)
    )
    where = jnp.stack([my_dp, my_core]).astype(jnp.int32)
    factor = ((right_eigen + epsilon) ** (-0.25))[:, None, :]
    spread = lax.all_to_all(pieces, "z", split_axis=0, concat_axis=0, tiled=True)
    spread, where, factor = lax.optimization_barrier((spread, where, factor))
    swapped = lax.ppermute(spread, "core", [(0, 1), (1, 0)])
    held = jnp.concatenate([t.reshape(n_z * blocks, 4 * 128) for t in (spread, swapped)])

    same = owner_map[:, None] == owner_map[None, :]
    order = jnp.arange(owner_map.shape[0], dtype=jnp.int32)
    slot = jnp.sum((same & (order[None, :] < order[:, None])).astype(jnp.int32), axis=1)
    place = jnp.where(owner_map % CORES == my_core, owner_map // CORES * cap + slot, -1)
    place = place.reshape(n_z, CORES, blocks)
    first, second = place[:, 0].reshape(-1), place[:, 1].reshape(-1)
    place = jnp.concatenate(
        [jnp.where(my_core == 0, first, second), jnp.where(my_core == 0, second, first)]
    )
    pick = (jnp.arange(n_z * cap, dtype=jnp.int32)[:, None] == place[None, :]).astype(jnp.bfloat16)
    chosen = jnp.dot(pick, held, preferred_element_type=jnp.float32).astype(jnp.bfloat16)
    deliver = chosen.reshape(n_z, cap, 4, 128)
    deliver, right_basis, factor = lax.optimization_barrier((deliver, right_basis, factor))
    middle = middle_step(right_basis, factor)
    arrived = lax.all_to_all(deliver, "z", split_axis=0, concat_axis=0, tiled=True)
    arrived, middle = lax.optimization_barrier((arrived, middle))

    owned = arrived.reshape(row_tiles, col_tiles, 2, cap, 4, 128)
    owned = owned.transpose(3, 0, 2, 4, 1, 5).reshape(cap, rows, width)
    n_opt = n_z * CORES
    line = broadcast_gather(owned, ALL, quads(n_opt))
    line, root = lax.optimization_barrier((line, root))
    squares = [line] + [swap_corner(line, a, b) for a, b in ((False, True), (True, False), (True, True))]

    update, left_new, right_new = slot_step(
        where, squares, stage(root), middle, left_stat, right_stat
    )
    return (update, left_new, right_new)


def solution(mesh):
    n_dp, n_opt = mesh.devices.shape
    inner = Mesh(mesh.devices.reshape(n_dp, n_opt // CORES, CORES), ALL)
    opt = ("z", "core")
    in_specs = (
        P("dp", opt, None, None),
        P(),
        P(opt, "dp", None),
        P(opt, None, None),
        P(opt, None),
        P(opt, "dp", None),
        P(opt, "dp", None),
    )
    out_specs = (P(opt, None, None), P(opt, "dp", None), P(opt, "dp", None))
    return jax.shard_map(body, mesh=inner, in_specs=in_specs, out_specs=out_specs, check_vma=False)
```

```python
import jax
import jax.numpy as jnp
from jax import lax
from jax.experimental import pallas as pl
from jax.experimental.pallas import tpu as pltpu
from jax.sharding import Mesh, PartitionSpec as P

decay_rate = 0.9
epsilon = 1e-06
CORES = 2
SIDE = 4
ALL = ("dp", "z", "core")
EVEN = ((0, 1), (2, 3))
ODD = ((1, 2), (0, 3))
MOVES = ((False, True), (True, False), (True, True))


def broadcast_gather(x, axis, groups=None):
    n = lax.axis_size(axis) if groups is None else len(groups[0])
    copies = jnp.broadcast_to(x[None], (n,) + x.shape)
    return lax.all_to_all(
        copies, axis, split_axis=0, concat_axis=0, tiled=True, axis_index_groups=groups
    )


def quads(n_opt):
    groups = []
    for opt in range(n_opt):
        pairs = EVEN if opt % CORES == 0 else ODD
        for across in pairs:
            for along in pairs:
                groups.append([(x * SIDE + y) * n_opt + opt for x in across for y in along])
    return groups


def swap_corner(x, across, along, parity):
    def partner(v, core, moved):
        return v if not moved else (SIDE - 1 - v if core == parity else v ^ 1)

    n_opt = lax.axis_size("z") * CORES
    pairs = []
    for source in range(SIDE * SIDE * n_opt):
        d, opt = divmod(source, n_opt)
        px = partner(d // SIDE, opt % CORES, across)
        py = partner(d % SIDE, opt % CORES, along)
        pairs.append((source, (px * SIDE + py) * n_opt + opt))
    return lax.ppermute(x, ALL, pairs)


def contract(a, b, dim_a, dim_b):
    return lax.dot_general(
        a, b, (((dim_a,), (dim_b,)), ((), ())), preferred_element_type=jnp.float32
    )


def slot_kernel(
    where, own4, along4, across4, corner4, root, middle, left, right,
    update, left_new, right_new,
    g, gram, update_out, left_out, right_out, update_sem, left_sem, right_sem
):
    my_dp, core = where[0], where[1]
    cap, rows, _ = left.shape
    my_x, my_y = my_dp // SIDE, my_dp % SIDE

    def spot(mine, moved, member):
        half = jnp.where(mine >= 2, 1, 0)
        outer = jnp.where((mine == 0) | (mine == SIDE - 1), 1, 0)
        if moved:
            half, outer = 1 - half, 1 - outer
        return jnp.where(core == 0, half * 2 + member, 2 + outer if member else 1 - outer)

    spots = {
        (step, member): pl.multiple_of(
            (spot(my_x, step // 2, member // 2) * SIDE + spot(my_y, step % 2, member % 2)) * rows,
            rows,
        )
        for step in range(SIDE)
        for member in range(SIDE)
    }
    group = 128 // rows
    own_rows = pl.ds(pl.multiple_of(my_dp * rows, rows), rows)
    lanes = pl.ds(pl.multiple_of(my_dp // group * 128, 128), 128)
    gram_rows = pl.ds(pl.multiple_of(my_dp % group * rows, rows), rows)
    results = []

    def send(source, target, sem, s):
        copy = pltpu.make_async_copy(source.at[s], target.at[s], sem.at[s])
        copy.start()
        results.append(copy)

    for s in range(cap):
        for step, rows4 in enumerate((own4, along4, across4, corner4)):
            for member in range(SIDE):
                g[s, pl.ds(spots[step, member], rows), :] = rows4[member, s]
        block = g[s]
        left_gram = contract(g[s, own_rows, :], block, 1, 1)
        left_out[s] = decay_rate * left[s] + (1.0 - decay_rate) * left_gram
        send(left_out, left_new, left_sem, s)
        gram[s] = contract(g[s, :, lanes], block, 0, 0)
        right_out[s] = decay_rate * right[s] + (1.0 - decay_rate) * gram[s, gram_rows, :]
        send(right_out, right_new, right_sem, s)
        applied = contract(root[s], block, 1, 0).astype(jnp.bfloat16)
        update_out[s] = contract(applied, middle[s], 1, 0).astype(jnp.bfloat16)
        send(update_out, update, update_sem, s)
    for copy in results:
        copy.wait()


def middle_kernel(basis, factor, middle):
    scaled = basis[0].astype(jnp.float32) * factor[0]
    high = scaled.astype(jnp.bfloat16)
    low = (scaled - high.astype(jnp.float32)).astype(jnp.bfloat16)
    product = contract(high, basis[0], 1, 1) + contract(low, basis[0], 1, 1)
    middle[0] = product.astype(jnp.bfloat16)


def middle_step(basis, factor):
    cap, width, _ = basis.shape
    whole = pl.BlockSpec((1, width, width), lambda s: (s, 0, 0))
    return pl.pallas_call(
        middle_kernel,
        grid=(cap,),
        in_specs=[whole, pl.BlockSpec((1, 1, width), lambda s: (s, 0, 0))],
        out_specs=whole,
        out_shape=jax.ShapeDtypeStruct(basis.shape, jnp.bfloat16),
        compiler_params=pltpu.CompilerParams(vmem_limit_bytes=58 * 1024 * 1024),
        cost_estimate=pl.CostEstimate(
            flops=4 * cap * width**3, bytes_accessed=4 * cap * width**2, transcendentals=0
        ),
    )(basis, factor)


def stage_kernel(where, own4, along4, across4, corner4, whole):
    my_dp, core = where[0], where[1]
    cap, rows = own4.shape[1], own4.shape[2]

    def moved(v, parity):
        return jnp.where(core == parity, SIDE - 1 - v, v + 1 - 2 * (v % 2))

    for outer, rows4 in enumerate((own4, along4, across4, corner4)):
        x, y = my_dp // SIDE, my_dp % SIDE
        x = moved(x, 0) if outer // 2 else x
        y = moved(y, 0) if outer % 2 else y
        for inner in range(SIDE):
            row = moved(x, 1) if inner // 2 else x
            column = moved(y, 1) if inner % 2 else y
            first = pl.multiple_of((row * SIDE + column) * rows, rows)
            for s in range(cap):
                whole[s, pl.ds(first, rows), :] = rows4[inner, s]


def stage(where, squares):
    _, cap, rows, width = squares[0].shape
    near = pl.BlockSpec(memory_space=pltpu.VMEM)
    return pl.pallas_call(
        stage_kernel,
        in_specs=[pl.BlockSpec(memory_space=pltpu.SMEM)] + [near] * 4,
        out_specs=near,
        out_shape=jax.ShapeDtypeStruct((cap, width, width), jnp.bfloat16),
        compiler_params=pltpu.CompilerParams(vmem_limit_bytes=32 * 1024 * 1024),
        cost_estimate=pl.CostEstimate(
            flops=0, bytes_accessed=4 * cap * width**2, transcendentals=0
        ),
    )(where, *squares)


def slot_step(where, squares, root, middle, left, right):
    cap, width, _ = middle.shape
    rows = left.shape[1]
    near = pl.BlockSpec(memory_space=pltpu.VMEM)
    away = pl.BlockSpec(memory_space=pl.ANY)
    return pl.pallas_call(
        slot_kernel,
        in_specs=[pl.BlockSpec(memory_space=pltpu.SMEM)] + [near] * 8,
        out_specs=[away] * 3,
        scratch_shapes=[
            pltpu.VMEM((cap, width, width), jnp.bfloat16),
            pltpu.VMEM((cap, 128, width), jnp.float32),
            pltpu.VMEM((cap, width, width), jnp.bfloat16),
            pltpu.VMEM(left.shape, jnp.float32),
            pltpu.VMEM(right.shape, jnp.float32),
        ]
        + [pltpu.SemaphoreType.DMA((cap,))] * 3,
        out_shape=[
            jax.ShapeDtypeStruct(middle.shape, jnp.bfloat16),
            jax.ShapeDtypeStruct(left.shape, jnp.float32),
            jax.ShapeDtypeStruct(right.shape, jnp.float32),
        ],
        compiler_params=pltpu.CompilerParams(vmem_limit_bytes=32 * 1024 * 1024),
        cost_estimate=pl.CostEstimate(
            flops=5 * cap * width**3, bytes_accessed=10 * cap * width**2, transcendentals=0
        ),
    )(where, *squares, root, middle, left, right)


def body(gradients, owner_map, left_root, right_basis, right_eigen, left_stat, right_stat):
    n_dp, n_z = lax.axis_size("dp"), lax.axis_size("z")
    _, blocks, width, _ = gradients.shape
    cap, rows, _ = left_stat.shape
    my_dp, my_core = lax.axis_index("dp"), lax.axis_index("core")
    row_tiles, col_tiles = rows // 8, width // 128

    sent = gradients.reshape(blocks, n_dp, rows, width).transpose(1, 0, 2, 3)
    sent, my_dp, my_core = lax.optimization_barrier((sent, my_dp, my_core))
    parts = lax.all_to_all(sent, "dp", split_axis=0, concat_axis=0, tiled=True)
    summed = jnp.sum(parts.astype(jnp.float32), axis=0).astype(jnp.bfloat16)

    summed = summed.reshape(blocks, row_tiles, 2, 4, col_tiles, 128)
    pieces = summed.transpose(1, 4, 2, 0, 3, 5).reshape(n_z, blocks * 4, 128)
    pieces, right_eigen, owner_map, my_dp, my_core, left_root = lax.optimization_barrier(
        (pieces, right_eigen, owner_map, my_dp, my_core, left_root)
    )
    root4 = jnp.stack([left_root] + [swap_corner(left_root, a, b, 1) for a, b in MOVES])
    where = jnp.stack([my_dp, my_core]).astype(jnp.int32)
    factor = ((right_eigen + epsilon) ** (-0.25))[:, None, :]
    spread = lax.all_to_all(pieces, "z", split_axis=0, concat_axis=0, tiled=True)
    spread, where, factor = lax.optimization_barrier((spread, where, factor))
    swapped = lax.ppermute(spread, "core", [(0, 1), (1, 0)])
    held = jnp.concatenate([t.reshape(n_z * blocks, 4 * 128) for t in (spread, swapped)])

    same = owner_map[:, None] == owner_map[None, :]
    order = jnp.arange(owner_map.shape[0], dtype=jnp.int32)
    slot = jnp.sum((same & (order[None, :] < order[:, None])).astype(jnp.int32), axis=1)
    place = jnp.where(owner_map % CORES == my_core, owner_map // CORES * cap + slot, -1)
    place = place.reshape(n_z, CORES, blocks)
    first, second = place[:, 0].reshape(-1), place[:, 1].reshape(-1)
    place = jnp.concatenate(
        [jnp.where(my_core == 0, first, second), jnp.where(my_core == 0, second, first)]
    )
    pick = (jnp.arange(n_z * cap, dtype=jnp.int32)[:, None] == place[None, :]).astype(jnp.bfloat16)
    chosen = jnp.dot(pick, held, preferred_element_type=jnp.float32).astype(jnp.bfloat16)
    deliver = chosen.reshape(n_z, cap, 4, 128)
    deliver, right_basis, factor, root4 = lax.optimization_barrier(
        (deliver, right_basis, factor, root4)
    )
    middle = middle_step(right_basis, factor)
    roots = [root4] + [swap_corner(root4, a, b, 0) for a, b in MOVES]
    arrived = lax.all_to_all(deliver, "z", split_axis=0, concat_axis=0, tiled=True)
    arrived, middle = lax.optimization_barrier((arrived, middle))

    owned = arrived.reshape(row_tiles, col_tiles, 2, cap, 4, 128)
    owned = owned.transpose(3, 0, 2, 4, 1, 5).reshape(cap, rows, width)
    n_opt = n_z * CORES
    line = broadcast_gather(owned, ALL, quads(n_opt))
    line, *roots = lax.optimization_barrier((line, *roots))
    squares = [line] + [swap_corner(line, a, b, 0) for a, b in MOVES]

    update, left_new, right_new = slot_step(
        where, squares, stage(where, roots), middle, left_stat, right_stat
    )
    return (update, left_new, right_new)


def solution(mesh):
    n_dp, n_opt = mesh.devices.shape
    inner = Mesh(mesh.devices.reshape(n_dp, n_opt // CORES, CORES), ALL)
    opt = ("z", "core")
    in_specs = (
        P("dp", opt, None, None),
        P(),
        P(opt, "dp", None),
        P(opt, None, None),
        P(opt, None),
        P(opt, "dp", None),
        P(opt, "dp", None),
    )
    out_specs = (P(opt, None, None), P(opt, "dp", None), P(opt, "dp", None))
    return jax.shard_map(body, mesh=inner, in_specs=in_specs, out_specs=out_specs, check_vma=False)
```

```python
import jax
import jax.numpy as jnp
from jax import lax
from jax.experimental import pallas as pl
from jax.experimental.pallas import tpu as pltpu
from jax.sharding import Mesh, PartitionSpec as P

decay_rate = 0.9
epsilon = 1e-06
CORES = 2
SIDE = 4
ALL = ("dp", "z", "core")
EVEN = ((0, 1), (2, 3))
ODD = ((1, 2), (0, 3))
MOVES = ((False, True), (True, False), (True, True))


def broadcast_gather(x, axis, groups=None):
    n = lax.axis_size(axis) if groups is None else len(groups[0])
    copies = jnp.broadcast_to(x[None], (n,) + x.shape)
    return lax.all_to_all(
        copies, axis, split_axis=0, concat_axis=0, tiled=True, axis_index_groups=groups
    )


def quads(n_opt):
    groups = []
    for opt in range(n_opt):
        pairs = EVEN if opt % CORES == 0 else ODD
        for across in pairs:
            for along in pairs:
                groups.append([(x * SIDE + y) * n_opt + opt for x in across for y in along])
    return groups


def swap_corner(x, across, along, parity):
    def partner(v, core, moved):
        return v if not moved else (SIDE - 1 - v if core == parity else v ^ 1)

    n_opt = lax.axis_size("z") * CORES
    pairs = []
    for source in range(SIDE * SIDE * n_opt):
        d, opt = divmod(source, n_opt)
        px = partner(d // SIDE, opt % CORES, across)
        py = partner(d % SIDE, opt % CORES, along)
        pairs.append((source, (px * SIDE + py) * n_opt + opt))
    return lax.ppermute(x, ALL, pairs)


def contract(a, b, dim_a, dim_b):
    return lax.dot_general(
        a, b, (((dim_a,), (dim_b,)), ((), ())), preferred_element_type=jnp.float32
    )


def slot_kernel(
    where, own4, along4, across4, corner4, root, middle, left, right,
    update, left_new, right_new,
    g, gram, update_out, left_out, right_out, update_sem, left_sem, right_sem
):
    my_dp, core = where[0], where[1]
    cap, rows, _ = left.shape
    my_x, my_y = my_dp // SIDE, my_dp % SIDE

    def spot(mine, moved, member):
        half = jnp.where(mine >= 2, 1, 0)
        outer = jnp.where((mine == 0) | (mine == SIDE - 1), 1, 0)
        if moved:
            half, outer = 1 - half, 1 - outer
        return jnp.where(core == 0, half * 2 + member, 2 + outer if member else 1 - outer)

    spots = {
        (step, member): pl.multiple_of(
            (spot(my_x, step // 2, member // 2) * SIDE + spot(my_y, step % 2, member % 2)) * rows,
            rows,
        )
        for step in range(SIDE)
        for member in range(SIDE)
    }
    group = 128 // rows
    own_rows = pl.ds(pl.multiple_of(my_dp * rows, rows), rows)
    lanes = pl.ds(pl.multiple_of(my_dp // group * 128, 128), 128)
    gram_rows = pl.ds(pl.multiple_of(my_dp % group * rows, rows), rows)
    results = []

    def send(source, target, sem, s):
        copy = pltpu.make_async_copy(source.at[s], target.at[s], sem.at[s])
        copy.start()
        results.append(copy)

    for s in range(cap):
        for step, rows4 in enumerate((own4, along4, across4, corner4)):
            for member in range(SIDE):
                g[s, pl.ds(spots[step, member], rows), :] = rows4[member, s]
        block = g[s]
        left_gram = contract(g[s, own_rows, :], block, 1, 1)
        left_out[s] = decay_rate * left[s] + (1.0 - decay_rate) * left_gram
        send(left_out, left_new, left_sem, s)
        gram[s] = contract(g[s, :, lanes], block, 0, 0)
        right_out[s] = decay_rate * right[s] + (1.0 - decay_rate) * gram[s, gram_rows, :]
        send(right_out, right_new, right_sem, s)
        applied = contract(root[s], block, 1, 0).astype(jnp.bfloat16)
        update_out[s] = contract(applied, middle[s], 1, 0).astype(jnp.bfloat16)
        send(update_out, update, update_sem, s)
    for copy in results:
        copy.wait()


def middle_kernel(basis, factor, middle):
    scaled = basis[0].astype(jnp.float32) * factor[0]
    high = scaled.astype(jnp.bfloat16)
    low = (scaled - high.astype(jnp.float32)).astype(jnp.bfloat16)
    product = contract(high, basis[0], 1, 1) + contract(low, basis[0], 1, 1)
    middle[0] = product.astype(jnp.bfloat16)


def middle_step(basis, factor):
    cap, width, _ = basis.shape
    whole = pl.BlockSpec((1, width, width), lambda s: (s, 0, 0))
    return pl.pallas_call(
        middle_kernel,
        grid=(cap,),
        in_specs=[whole, pl.BlockSpec((1, 1, width), lambda s: (s, 0, 0))],
        out_specs=whole,
        out_shape=jax.ShapeDtypeStruct(basis.shape, jnp.bfloat16),
        compiler_params=pltpu.CompilerParams(vmem_limit_bytes=58 * 1024 * 1024),
        cost_estimate=pl.CostEstimate(
            flops=4 * cap * width**3, bytes_accessed=4 * cap * width**2, transcendentals=0
        ),
    )(basis, factor)


def stage_kernel(where, own4, along4, across4, corner4, whole):
    my_dp, core = where[0], where[1]
    cap, rows = own4.shape[1], own4.shape[2]

    def moved(v, parity):
        return jnp.where(core == parity, SIDE - 1 - v, v + 1 - 2 * (v % 2))

    for outer, rows4 in enumerate((own4, along4, across4, corner4)):
        x, y = my_dp // SIDE, my_dp % SIDE
        x = moved(x, 0) if outer // 2 else x
        y = moved(y, 0) if outer % 2 else y
        for inner in range(SIDE):
            row = moved(x, 1) if inner // 2 else x
            column = moved(y, 1) if inner % 2 else y
            first = pl.multiple_of((row * SIDE + column) * rows, rows)
            for s in range(cap):
                whole[s, pl.ds(first, rows), :] = rows4[inner, s]


def stage(where, squares):
    _, cap, rows, width = squares[0].shape
    near = pl.BlockSpec(memory_space=pltpu.VMEM)
    return pl.pallas_call(
        stage_kernel,
        in_specs=[pl.BlockSpec(memory_space=pltpu.SMEM)] + [near] * 4,
        out_specs=near,
        out_shape=jax.ShapeDtypeStruct((cap, width, width), jnp.bfloat16),
        compiler_params=pltpu.CompilerParams(vmem_limit_bytes=32 * 1024 * 1024),
        cost_estimate=pl.CostEstimate(
            flops=0, bytes_accessed=4 * cap * width**2, transcendentals=0
        ),
    )(where, *squares)


def slot_step(where, squares, root, middle, left, right):
    cap, width, _ = middle.shape
    rows = left.shape[1]
    near = pl.BlockSpec(memory_space=pltpu.VMEM)
    away = pl.BlockSpec(memory_space=pl.ANY)
    return pl.pallas_call(
        slot_kernel,
        in_specs=[pl.BlockSpec(memory_space=pltpu.SMEM)] + [near] * 8,
        out_specs=[away] * 3,
        scratch_shapes=[
            pltpu.VMEM((cap, width, width), jnp.bfloat16),
            pltpu.VMEM((cap, 128, width), jnp.float32),
            pltpu.VMEM((cap, width, width), jnp.bfloat16),
            pltpu.VMEM(left.shape, jnp.float32),
            pltpu.VMEM(right.shape, jnp.float32),
        ]
        + [pltpu.SemaphoreType.DMA((cap,))] * 3,
        out_shape=[
            jax.ShapeDtypeStruct(middle.shape, jnp.bfloat16),
            jax.ShapeDtypeStruct(left.shape, jnp.float32),
            jax.ShapeDtypeStruct(right.shape, jnp.float32),
        ],
        compiler_params=pltpu.CompilerParams(vmem_limit_bytes=32 * 1024 * 1024),
        cost_estimate=pl.CostEstimate(
            flops=5 * cap * width**3, bytes_accessed=10 * cap * width**2, transcendentals=0
        ),
    )(where, *squares, root, middle, left, right)


def body(gradients, owner_map, left_root, right_basis, right_eigen, left_stat, right_stat):
    n_dp, n_z = lax.axis_size("dp"), lax.axis_size("z")
    _, blocks, width, _ = gradients.shape
    cap, rows, _ = left_stat.shape
    my_dp, my_core = lax.axis_index("dp"), lax.axis_index("core")
    row_tiles, col_tiles = rows // 8, width // 128

    sent = gradients.reshape(blocks, n_dp, rows, width).transpose(1, 0, 2, 3)
    sent, my_dp, my_core = lax.optimization_barrier((sent, my_dp, my_core))
    parts = lax.all_to_all(sent, "dp", split_axis=0, concat_axis=0, tiled=True)
    summed = jnp.sum(parts.astype(jnp.float32), axis=0).astype(jnp.bfloat16)

    summed = summed.reshape(blocks, row_tiles, 2, 4, col_tiles, 128)
    pieces = summed.transpose(1, 4, 2, 0, 3, 5).reshape(n_z, blocks * 4, 128)
    pieces, right_eigen, owner_map, my_dp, my_core, left_root = lax.optimization_barrier(
        (pieces, right_eigen, owner_map, my_dp, my_core, left_root)
    )
    root4 = jnp.stack([left_root] + [swap_corner(left_root, a, b, 1) for a, b in MOVES])
    where = jnp.stack([my_dp, my_core]).astype(jnp.int32)
    factor = ((right_eigen + epsilon) ** (-0.25))[:, None, :]
    spread = lax.all_to_all(pieces, "z", split_axis=0, concat_axis=0, tiled=True)
    spread, where, factor = lax.optimization_barrier((spread, where, factor))
    swapped = lax.ppermute(spread, "core", [(0, 1), (1, 0)])
    held = jnp.concatenate([t.reshape(n_z * blocks, 4 * 128) for t in (spread, swapped)])

    same = owner_map[:, None] == owner_map[None, :]
    order = jnp.arange(owner_map.shape[0], dtype=jnp.int32)
    slot = jnp.sum((same & (order[None, :] < order[:, None])).astype(jnp.int32), axis=1)
    place = jnp.where(owner_map % CORES == my_core, owner_map // CORES * cap + slot, -1)
    place = place.reshape(n_z, CORES, blocks)
    first, second = place[:, 0].reshape(-1), place[:, 1].reshape(-1)
    place = jnp.concatenate(
        [jnp.where(my_core == 0, first, second), jnp.where(my_core == 0, second, first)]
    )
    pick = (jnp.arange(n_z * cap, dtype=jnp.int32)[:, None] == place[None, :]).astype(jnp.bfloat16)
    chosen = jnp.dot(pick, held, preferred_element_type=jnp.float32).astype(jnp.bfloat16)
    deliver = chosen.reshape(n_z, cap, 4, 128)
    deliver, right_basis, factor = lax.optimization_barrier((deliver, right_basis, factor))
    middle = middle_step(right_basis, factor)
    roots = [root4] + [swap_corner(root4, a, b, 0) for a, b in MOVES]
    arrived = lax.all_to_all(deliver, "z", split_axis=0, concat_axis=0, tiled=True)
    arrived, middle = lax.optimization_barrier((arrived, middle))

    owned = arrived.reshape(row_tiles, col_tiles, 2, cap, 4, 128)
    owned = owned.transpose(3, 0, 2, 4, 1, 5).reshape(cap, rows, width)
    n_opt = n_z * CORES
    line = broadcast_gather(owned, ALL, quads(n_opt))
    line, *roots = lax.optimization_barrier((line, *roots))
    squares = [line] + [swap_corner(line, a, b, 0) for a, b in MOVES]

    update, left_new, right_new = slot_step(
        where, squares, stage(where, roots), middle, left_stat, right_stat
    )
    return (update, left_new, right_new)


def solution(mesh):
    n_dp, n_opt = mesh.devices.shape
    inner = Mesh(mesh.devices.reshape(n_dp, n_opt // CORES, CORES), ALL)
    opt = ("z", "core")
    in_specs = (
        P("dp", opt, None, None),
        P(),
        P(opt, "dp", None),
        P(opt, None, None),
        P(opt, None),
        P(opt, "dp", None),
        P(opt, "dp", None),
    )
    out_specs = (P(opt, None, None), P(opt, "dp", None), P(opt, "dp", None))
    return jax.shard_map(body, mesh=inner, in_specs=in_specs, out_specs=out_specs, check_vma=False)
```

```python
import jax
import jax.numpy as jnp
from jax import lax
from jax.experimental import pallas as pl
from jax.experimental.pallas import tpu as pltpu
from jax.sharding import Mesh, PartitionSpec as P

decay_rate = 0.9
epsilon = 1e-06
CORES = 2
SIDE = 4
ALL = ("dp", "z", "core")
EVEN = ((0, 1), (2, 3))
ODD = ((1, 2), (0, 3))
MOVES = ((False, True), (True, False), (True, True))


def broadcast_gather(x, axis, groups=None):
    n = lax.axis_size(axis) if groups is None else len(groups[0])
    copies = jnp.broadcast_to(x[None], (n,) + x.shape)
    return lax.all_to_all(
        copies, axis, split_axis=0, concat_axis=0, tiled=True, axis_index_groups=groups
    )


def quads(n_opt):
    groups = []
    for opt in range(n_opt):
        pairs = EVEN if opt % CORES == 0 else ODD
        for across in pairs:
            for along in pairs:
                groups.append([(x * SIDE + y) * n_opt + opt for x in across for y in along])
    return groups


def swap_corner(x, across, along, parity):
    def partner(v, core, moved):
        return v if not moved else (SIDE - 1 - v if core == parity else v ^ 1)

    n_opt = lax.axis_size("z") * CORES
    pairs = []
    for source in range(SIDE * SIDE * n_opt):
        d, opt = divmod(source, n_opt)
        px = partner(d // SIDE, opt % CORES, across)
        py = partner(d % SIDE, opt % CORES, along)
        pairs.append((source, (px * SIDE + py) * n_opt + opt))
    return lax.ppermute(x, ALL, pairs)


def contract(a, b, dim_a, dim_b):
    return lax.dot_general(
        a, b, (((dim_a,), (dim_b,)), ((), ())), preferred_element_type=jnp.float32
    )


def slot_kernel(
    where, own4, along4, across4, corner4, root, middle, left, right,
    update, left_new, right_new,
    g, gram, update_out, left_out, right_out, update_sem, left_sem, right_sem
):
    my_dp, core = where[0], where[1]
    cap, rows, _ = left.shape
    my_x, my_y = my_dp // SIDE, my_dp % SIDE

    def spot(mine, moved, member):
        half = jnp.where(mine >= 2, 1, 0)
        outer = jnp.where((mine == 0) | (mine == SIDE - 1), 1, 0)
        if moved:
            half, outer = 1 - half, 1 - outer
        return jnp.where(core == 0, half * 2 + member, 2 + outer if member else 1 - outer)

    spots = {
        (step, member): pl.multiple_of(
            (spot(my_x, step // 2, member // 2) * SIDE + spot(my_y, step % 2, member % 2)) * rows,
            rows,
        )
        for step in range(SIDE)
        for member in range(SIDE)
    }
    group = 128 // rows
    own_rows = pl.ds(pl.multiple_of(my_dp * rows, rows), rows)
    lanes = pl.ds(pl.multiple_of(my_dp // group * 128, 128), 128)
    gram_rows = pl.ds(pl.multiple_of(my_dp % group * rows, rows), rows)
    results = []

    def send(source, target, sem, s):
        copy = pltpu.make_async_copy(source.at[s], target.at[s], sem.at[s])
        copy.start()
        results.append(copy)

    for s in range(cap):
        for step, rows4 in enumerate((own4, along4, across4, corner4)):
            for member in range(SIDE):
                g[s, pl.ds(spots[step, member], rows), :] = rows4[member, s]
        block = g[s]
        left_gram = contract(g[s, own_rows, :], block, 1, 1)
        left_out[s] = decay_rate * left[s] + (1.0 - decay_rate) * left_gram
        send(left_out, left_new, left_sem, s)
        gram[s] = contract(g[s, :, lanes], block, 0, 0)
        right_out[s] = decay_rate * right[s] + (1.0 - decay_rate) * gram[s, gram_rows, :]
        send(right_out, right_new, right_sem, s)
        applied = contract(root[s], block, 1, 0).astype(jnp.bfloat16)
        update_out[s] = contract(applied, middle[s], 1, 0).astype(jnp.bfloat16)
        send(update_out, update, update_sem, s)
    for copy in results:
        copy.wait()


def middle_kernel(basis, factor, middle):
    scaled = basis[0].astype(jnp.float32) * factor[0]
    high = scaled.astype(jnp.bfloat16)
    low = (scaled - high.astype(jnp.float32)).astype(jnp.bfloat16)
    product = contract(high, basis[0], 1, 1) + contract(low, basis[0], 1, 1)
    middle[0] = product.astype(jnp.bfloat16)


def middle_step(basis, factor):
    cap, width, _ = basis.shape
    whole = pl.BlockSpec((1, width, width), lambda s: (s, 0, 0))
    return pl.pallas_call(
        middle_kernel,
        grid=(cap,),
        in_specs=[whole, pl.BlockSpec((1, 1, width), lambda s: (s, 0, 0))],
        out_specs=whole,
        out_shape=jax.ShapeDtypeStruct(basis.shape, jnp.bfloat16),
        compiler_params=pltpu.CompilerParams(vmem_limit_bytes=58 * 1024 * 1024),
        cost_estimate=pl.CostEstimate(
            flops=4 * cap * width**3, bytes_accessed=4 * cap * width**2, transcendentals=0
        ),
    )(basis, factor)


def stage_kernel(where, own4, along4, across4, corner4, whole):
    my_dp, core = where[0], where[1]
    cap, rows = own4.shape[1], own4.shape[2]

    def moved(v, parity):
        return jnp.where(core == parity, SIDE - 1 - v, v + 1 - 2 * (v % 2))

    for outer, rows4 in enumerate((own4, along4, across4, corner4)):
        x, y = my_dp // SIDE, my_dp % SIDE
        x = moved(x, 0) if outer // 2 else x
        y = moved(y, 0) if outer % 2 else y
        for inner in range(SIDE):
            row = moved(x, 1) if inner // 2 else x
            column = moved(y, 1) if inner % 2 else y
            first = pl.multiple_of((row * SIDE + column) * rows, rows)
            for s in range(cap):
                whole[s, pl.ds(first, rows), :] = rows4[inner, s]


def stage(where, squares):
    _, cap, rows, width = squares[0].shape
    near = pl.BlockSpec(memory_space=pltpu.VMEM)
    return pl.pallas_call(
        stage_kernel,
        in_specs=[pl.BlockSpec(memory_space=pltpu.SMEM)] + [near] * 4,
        out_specs=near,
        out_shape=jax.ShapeDtypeStruct((cap, width, width), jnp.bfloat16),
        compiler_params=pltpu.CompilerParams(vmem_limit_bytes=32 * 1024 * 1024),
        cost_estimate=pl.CostEstimate(
            flops=0, bytes_accessed=4 * cap * width**2, transcendentals=0
        ),
    )(where, *squares)


def slot_step(where, squares, root, middle, left, right):
    cap, width, _ = middle.shape
    rows = left.shape[1]
    near = pl.BlockSpec(memory_space=pltpu.VMEM)
    away = pl.BlockSpec(memory_space=pl.ANY)
    return pl.pallas_call(
        slot_kernel,
        in_specs=[pl.BlockSpec(memory_space=pltpu.SMEM)] + [near] * 8,
        out_specs=[away] * 3,
        scratch_shapes=[
            pltpu.VMEM((cap, width, width), jnp.bfloat16),
            pltpu.VMEM((cap, 128, width), jnp.float32),
            pltpu.VMEM((cap, width, width), jnp.bfloat16),
            pltpu.VMEM(left.shape, jnp.float32),
            pltpu.VMEM(right.shape, jnp.float32),
        ]
        + [pltpu.SemaphoreType.DMA((cap,))] * 3,
        out_shape=[
            jax.ShapeDtypeStruct(middle.shape, jnp.bfloat16),
            jax.ShapeDtypeStruct(left.shape, jnp.float32),
            jax.ShapeDtypeStruct(right.shape, jnp.float32),
        ],
        compiler_params=pltpu.CompilerParams(vmem_limit_bytes=32 * 1024 * 1024),
        cost_estimate=pl.CostEstimate(
            flops=5 * cap * width**3, bytes_accessed=10 * cap * width**2, transcendentals=0
        ),
    )(where, *squares, root, middle, left, right)


def body(gradients, owner_map, left_root, right_basis, right_eigen, left_stat, right_stat):
    n_dp, n_z = lax.axis_size("dp"), lax.axis_size("z")
    _, blocks, width, _ = gradients.shape
    cap, rows, _ = left_stat.shape
    my_dp, my_core = lax.axis_index("dp"), lax.axis_index("core")
    row_tiles, col_tiles = rows // 8, width // 128

    sent = gradients.reshape(blocks, n_dp, rows, width).transpose(1, 0, 2, 3)
    sent, my_dp, my_core = lax.optimization_barrier((sent, my_dp, my_core))
    parts = lax.all_to_all(sent, "dp", split_axis=0, concat_axis=0, tiled=True)
    summed = jnp.sum(parts.astype(jnp.float32), axis=0).astype(jnp.bfloat16)

    summed = summed.reshape(blocks, row_tiles, 2, 4, col_tiles, 128)
    pieces = summed.transpose(1, 4, 2, 0, 3, 5).reshape(n_z, blocks * 4, 128)
    pieces, left_root = lax.optimization_barrier((pieces, left_root))
    root4 = jnp.stack([left_root] + [swap_corner(left_root, a, b, 1) for a, b in MOVES])
    spread = lax.all_to_all(pieces, "z", split_axis=0, concat_axis=0, tiled=True)
    spread, owner_map, my_core = lax.optimization_barrier((spread, owner_map, my_core))
    swapped = lax.ppermute(spread, "core", [(0, 1), (1, 0)])
    held = jnp.concatenate([t.reshape(n_z * blocks, 4 * 128) for t in (spread, swapped)])

    same = owner_map[:, None] == owner_map[None, :]
    order = jnp.arange(owner_map.shape[0], dtype=jnp.int32)
    slot = jnp.sum((same & (order[None, :] < order[:, None])).astype(jnp.int32), axis=1)
    place = jnp.where(owner_map % CORES == my_core, owner_map // CORES * cap + slot, -1)
    place = place.reshape(n_z, CORES, blocks)
    first, second = place[:, 0].reshape(-1), place[:, 1].reshape(-1)
    place = jnp.concatenate(
        [jnp.where(my_core == 0, first, second), jnp.where(my_core == 0, second, first)]
    )
    pick = (jnp.arange(n_z * cap, dtype=jnp.int32)[:, None] == place[None, :]).astype(jnp.bfloat16)
    chosen = jnp.dot(pick, held, preferred_element_type=jnp.float32).astype(jnp.bfloat16)
    deliver = chosen.reshape(n_z, cap, 4, 128)
    deliver, right_basis, right_eigen, my_dp, my_core = lax.optimization_barrier(
        (deliver, right_basis, right_eigen, my_dp, my_core)
    )
    where = jnp.stack([my_dp, my_core]).astype(jnp.int32)
    factor = ((right_eigen + epsilon) ** (-0.25))[:, None, :]
    middle = middle_step(right_basis, factor)
    roots = [root4] + [swap_corner(root4, a, b, 0) for a, b in MOVES]
    arrived = lax.all_to_all(deliver, "z", split_axis=0, concat_axis=0, tiled=True)
    arrived, middle, where = lax.optimization_barrier((arrived, middle, where))

    owned = arrived.reshape(row_tiles, col_tiles, 2, cap, 4, 128)
    owned = owned.transpose(3, 0, 2, 4, 1, 5).reshape(cap, rows, width)
    n_opt = n_z * CORES
    line = broadcast_gather(owned, ALL, quads(n_opt))
    line, *roots = lax.optimization_barrier((line, *roots))
    squares = [line] + [swap_corner(line, a, b, 0) for a, b in MOVES]

    update, left_new, right_new = slot_step(
        where, squares, stage(where, roots), middle, left_stat, right_stat
    )
    return (update, left_new, right_new)


def solution(mesh):
    n_dp, n_opt = mesh.devices.shape
    inner = Mesh(mesh.devices.reshape(n_dp, n_opt // CORES, CORES), ALL)
    opt = ("z", "core")
    in_specs = (
        P("dp", opt, None, None),
        P(),
        P(opt, "dp", None),
        P(opt, None, None),
        P(opt, None),
        P(opt, "dp", None),
        P(opt, "dp", None),
    )
    out_specs = (P(opt, None, None), P(opt, "dp", None), P(opt, "dp", None))
    return jax.shard_map(body, mesh=inner, in_specs=in_specs, out_specs=out_specs, check_vma=False)
```
